128 devices in a mesh: ctx: 32 (over y, x, core), head: 4 (over z).
Axes of the slice: x: 4, y: 4, z: 4, core: 2. Of those that a mesh axis runs over, the one named last changes fastest.
Arguments:
- q_lin: float32 [8192, 4096], P('ctx', 'head'), may hold values from -6 to 6
- k_lin: float32 [8192, 4096], P('ctx', 'head'), may hold values from -0.9722718 to 0.9722718
- v_lin: float32 [8192, 4096], P('ctx', 'head'), may hold values from -201 to 201
- log_decay: float32 [32, 8192], P('head', 'ctx'), may hold values from -1 to 0
- lin_gain: float32 [4096], P('head'), may hold values from 0.1 to 1.9
- q_soft: float32 [8192, 6144], P('ctx', 'head'), may hold values from -36 to 36
- k_soft: float32 [8192, 1024], P('ctx', 'head'), may hold values from -4 to 4
- v_soft: float32 [8192, 1024], P('ctx', 'head'), may hold values from -6 to 6
Outputs:
- lin_out: float32 [8192, 4096], P('ctx', 'head')
- soft_out: float32 [8192, 6144], P('ctx', 'head')
The draws below stay inside these ranges and needn't reach their ends.
All inputs are finite; a program needn't handle non-finite values.
Results may differ from the reference program's by a relative error of at most 0.0003.
Values sent between devices are 32-bit elements; how exact they have to be, the bound alone decides.
A program may use at most 128 MiB of HBM per device.

```python
import math
import jax
import jax.numpy as jnp
from jax import lax

HD = 128
LH = 32
QH = 48
KVH = 8
TOK_DEV = 256
WINDOW_TOKENS = 8192


def decay_rates(key, slow_share):
    key = jax.random.fold_in(key, 21)
    class_key, rapid_key, gentle_key = jax.random.split(key, 3)
    slow_heads = jax.random.uniform(class_key, (LH, 1), jnp.float32) < slow_share
    fast_rate = jax.random.uniform(rapid_key, (LH, 1), jnp.float32, 1.0 / 50.0, 1.0 / 30.0)
    slow_rate = jax.random.uniform(gentle_key, (LH, 1), jnp.float32, 0.1, 0.8) / WINDOW_TOKENS
    return jnp.where(slow_heads, slow_rate, fast_rate)


def draw_k_soft(key, part):
    key = jax.random.fold_in(key, 11)
    base_keys = jax.random.truncated_normal(key, -4.0, 4.0, (WINDOW_TOKENS, KVH, HD), jnp.float32)
    result = base_keys
    return result.reshape(WINDOW_TOKENS, KVH * HD)


def draw_q_soft(key, part):
    key = jax.random.fold_in(key, 12)
    shape = (WINDOW_TOKENS, KVH, QH // KVH, HD)
    result = 2.0 * jax.random.truncated_normal(key, -4.0, 4.0, shape, jnp.float32)
    return result.reshape(WINDOW_TOKENS, QH * HD)


def draw_log_decay(key, part):
    slow_share = 0.6
    head_decay_rate = decay_rates(key, slow_share)
    key = jax.random.fold_in(key, 13)
    block_seed_key, cell_seed_key, spike_key, dropped_key = jax.random.split(key, 4)
    block_multiplier = jnp.exp(jax.random.uniform(block_seed_key, (LH, WINDOW_TOKENS // TOK_DEV, 1), jnp.float32, -0.5, 0.5))
    block_multiplier = jnp.broadcast_to(block_multiplier, (LH, WINDOW_TOKENS // TOK_DEV, TOK_DEV)).reshape(LH, WINDOW_TOKENS)
    cell_multiplier = jax.random.uniform(cell_seed_key, (LH, WINDOW_TOKENS), jnp.float32, 0.5, 1.5)
    spike_positions = jax.random.randint(spike_key, (3,), 0, WINDOW_TOKENS)
    spike_values = jnp.any(jnp.arange(WINDOW_TOKENS)[None, :] == spike_positions[:, None], axis=0)[None, :]
    dropped_entries = jax.random.uniform(dropped_key, (1, WINDOW_TOKENS), jnp.float32, 0.22, 0.69)
    return -head_decay_rate * block_multiplier * cell_multiplier - jnp.where(spike_values, dropped_entries, 0.0)


def draw_v_lin(key, part):
    slow_share = 0.6
    head_decay_rate = decay_rates(key, slow_share)
    key = jax.random.fold_in(key, 14)
    value_key, column_key, row_key = jax.random.split(key, 3)
    memory_scale = jnp.repeat(jnp.sqrt(jnp.minimum(1.0, 48.0 * head_decay_rate[:, 0])), HD)[None, :]
    column_scale = jnp.exp(jax.random.uniform(column_key, (1, LH * HD), jnp.float32, math.log(0.3), math.log(3.0)))
    row_scale = jnp.exp(jax.random.uniform(row_key, (WINDOW_TOKENS, 1), jnp.float32, math.log(0.5), math.log(5.0)))
    head_share = (jnp.arange(LH * HD) // HD).astype(jnp.float32)[None, :] / (LH - 1)
    head_scale = jnp.power(3.0, head_share)
    base_rows = jax.random.truncated_normal(value_key, -4.0, 4.0, (WINDOW_TOKENS, LH * HD), jnp.float32)
    return base_rows * head_scale * column_scale * row_scale * memory_scale


def draw_q_lin(key, part):
    key = jax.random.fold_in(key, 15)
    value_key, picked_key, depth_key = jax.random.split(key, 3)
    shape = (WINDOW_TOKENS, LH * HD)
    base_rows = jax.random.truncated_normal(value_key, -6.0, 6.0, shape, jnp.float32)
    picked = jax.random.uniform(picked_key, (WINDOW_TOKENS, 1), jnp.float32) < 1.0 / 16.0
    depth_scale = jnp.power(10.0, jax.random.uniform(depth_key, (WINDOW_TOKENS, 1), jnp.float32, -5.0, -1.0))
    return base_rows * jnp.where(picked, depth_scale, 1.0)


def draw_k_lin(key, part):
    key = jax.random.fold_in(key, 16)
    value_key, loudness_key = jax.random.split(key, 2)
    shape = (WINDOW_TOKENS, LH * HD)
    group_count = WINDOW_TOKENS // 8 + 1
    loudness = jnp.exp(jax.random.uniform(loudness_key, (group_count, LH), jnp.float32, -2.0, 1.0))
    loudness_rows = jnp.repeat(loudness[jnp.arange(WINDOW_TOKENS) // 8], HD, axis=1)
    base_rows = jax.random.truncated_normal(value_key, -4.0, 4.0, shape, jnp.float32)
    return base_rows * loudness_rows / math.sqrt(HD)


def level_of(stream_key, shape, pieces, smallest, top_value):
    level, own = 1.0, jax.random.fold_in(stream_key, 6)
    for axis_at, blocks in pieces:
        steps = jnp.exp(jax.random.uniform(jax.random.fold_in(own, axis_at), (blocks,), jnp.float32, smallest / len(pieces), top_value / len(pieces)))
        level = level * jnp.repeat(steps, shape[axis_at] // blocks).reshape([-1 if axis == axis_at else 1 for axis in range(len(shape))])
    return level


def normal_values(rng, extent, spread, limit, pieces=(), kind=jnp.bfloat16):
    values = spread * jax.random.normal(rng, extent, jnp.float32)
    if pieces:
        values = values * level_of(rng, extent, pieces, -0.22, 0.18)
    return jnp.clip(values, -limit, limit).astype(kind)


def setup_inputs(seed: int = 0) -> dict:
    key_of = jax.random.split(jax.random.key(seed), 9)
    return {
        "q_lin": draw_q_lin(jax.random.fold_in(key_of[8], 71), 0),
        "k_lin": draw_k_lin(jax.random.fold_in(key_of[8], 71), 0),
        "v_lin": draw_v_lin(jax.random.fold_in(key_of[8], 71), 0),
        "log_decay": draw_log_decay(jax.random.fold_in(key_of[8], 71), 0),
        "lin_gain": jnp.clip(1.0 + 0.18 * jax.random.normal(key_of[4], (LH * HD,), jnp.float32), 0.1, 1.9),
        "q_soft": draw_q_soft(jax.random.fold_in(key_of[8], 71), 0),
        "k_soft": draw_k_soft(jax.random.fold_in(key_of[8], 71), 0),
        "v_soft": normal_values(key_of[7], (WINDOW_TOKENS, KVH * HD), 1.0, 6.0, ((0, 32), (1, 4)), jnp.float32),
    }


HIGHEST = lax.Precision.HIGHEST
EPSILON = 1e-05

def block_terms(queries, key_rows, value_rows, log_rates):
    length = queries.shape[0]
    cumulative = jnp.cumsum(log_rates, axis=1)
    positions = jnp.arange(length)
    causal = (positions[:, None] >= positions[None, :])[None]
    decay_gaps = cumulative[:, :, None] - cumulative[:, None, :]
    weights = jnp.where(causal, jnp.exp(jnp.where(causal, decay_gaps, 0.0)), 0.0)
    scores = jnp.einsum('thd,shd->hts', queries, key_rows, precision=HIGHEST)
    inside = jnp.einsum('hts,shd->thd', scores * weights, value_rows, precision=HIGHEST)
    block_total = cumulative[:, -1]
    trailing = jnp.exp(block_total[:, None] - cumulative)
    scaled_keys = key_rows * jnp.transpose(trailing)[:, :, None]
    local_state = jnp.einsum('shd,she->hde', scaled_keys, value_rows, precision=HIGHEST)
    leading = jnp.transpose(jnp.exp(cumulative))[:, :, None]
    return (inside, leading, block_total, local_state)

def lightning(q_lin, k_lin, v_lin, log_decay):
    head_count = log_decay.shape[0]
    block_count = WINDOW_TOKENS // TOK_DEV

    def by_block(array):
        return array.reshape(block_count, TOK_DEV, head_count, HD)
    rates = jnp.transpose(log_decay.reshape(head_count, block_count, TOK_DEV), (1, 0, 2))

    def advance(carried, operands):
        queries, key_rows, value_rows, log_rates = operands
        inside, leading, block_total, local_state = block_terms(queries, key_rows, value_rows, log_rates)
        result = inside + leading * jnp.einsum('thd,hde->the', queries, carried, precision=HIGHEST)
        carried = jnp.exp(block_total)[:, None, None] * carried + local_state
        return (carried, result)
    initial = jnp.zeros((head_count, HD, HD), jnp.float32)
    _, outputs = lax.scan(advance, initial, (by_block(q_lin), by_block(k_lin), by_block(v_lin), rates))
    return outputs.reshape(WINDOW_TOKENS, head_count * HD)

def softmax_layer(q_soft, k_soft, v_soft):
    group_size = QH // KVH
    block_count = WINDOW_TOKENS // TOK_DEV
    score_scale = 1.0 / math.sqrt(HD)
    query_blocks = jnp.transpose(q_soft.reshape(block_count, TOK_DEV, KVH, group_size, HD), (2, 0, 3, 1, 4))
    key_heads = jnp.transpose(k_soft.reshape(WINDOW_TOKENS, KVH, HD), (1, 0, 2))
    value_heads = jnp.transpose(v_soft.reshape(WINDOW_TOKENS, KVH, HD), (1, 0, 2))
    positions = jnp.arange(WINDOW_TOKENS)
    starts = jnp.arange(block_count) * TOK_DEV

    def per_head(operands):
        head_queries, head_keys, head_values = operands

        def per_block(block_operands):
            block_queries, first_row = block_operands
            scores = jnp.einsum('gtd,sd->gts', block_queries, head_keys, precision=HIGHEST) * score_scale
            query_pos = first_row + jnp.arange(TOK_DEV)
            visible = (positions[None, :] <= query_pos[:, None])[None]
            scores = jnp.where(visible, scores, -jnp.inf)
            row_peak = lax.optimization_barrier(jnp.max(scores, axis=2, keepdims=True))
            weights = jnp.exp(scores - row_peak)
            summed = jnp.einsum('gts,sd->gtd', weights, head_values, precision=HIGHEST)
            return summed / lax.optimization_barrier(jnp.sum(weights, axis=2, keepdims=True))
        return lax.map(per_block, (head_queries, starts))
    merged = lax.map(per_head, (query_blocks, key_heads, value_heads))
    return jnp.transpose(merged, (1, 3, 0, 2, 4)).reshape(WINDOW_TOKENS, QH * HD)

def reference(q_lin, k_lin, v_lin, log_decay, lin_gain, q_soft, k_soft, v_soft):
    linear = lightning(q_lin, k_lin, v_lin, log_decay)
    energy = lax.optimization_barrier(jnp.sum(linear * linear, axis=1, keepdims=True))
    lin_out = linear * lax.rsqrt(energy / (LH * HD) + EPSILON) * lin_gain
    soft_out = softmax_layer(q_soft, k_soft, v_soft)
    return (lin_out, soft_out)
```

```python
import functools
import math

import jax
import jax.numpy as jnp
from jax import lax
from jax.experimental import pallas as pl
from jax.experimental.pallas import tpu as pltpu
from jax.sharding import PartitionSpec as P

HD = 128
LH = 32
EPSILON = 1e-05
NEGATIVE = -1e30
F32 = jnp.float32
BF16 = jnp.bfloat16
NT = (((1,), (1,)), ((), ()))
TN = (((0,), (0,)), ((), ()))
ROWS = 256
KEYS = 512
GROUP = 6
TILES = GROUP * ROWS
NEAR = ((0, 0), (2, 0), (0, 3), (0, 1), (2, 3), (2, 1), (0, 2), (2, 2))


def halves(value):
    high = value.astype(BF16)
    return high, (value - high.astype(F32)).astype(BF16)


def dot3(left, right, dims):
    (la,), (ra,) = dims[0]
    lh, ll = halves(left)
    rh, rl = halves(right)
    return lax.dot_general(
        jnp.concatenate([lh, ll, lh], la),
        jnp.concatenate([rh, rh, rl], ra),
        dims,
        preferred_element_type=F32,
    )


def kernel(
    q_lin, k_lin, v_lin, log_decay, gain, q_soft, k_soft, v_soft,
    lin_out, soft_out,
    kv, kv_out, q_in, q3, k3, v2, m_all, l_all, acc, o_send,
    local, gathered, prior, entering, energy, energy_in, cum_row, cum_col,
    swap_send, swap_recv, send, recv, o_ss, o_rs, l_ss, l_rs, e_ss, e_rs, n_ss, n_rs,
):
    me = lax.axis_index("ctx")
    z = lax.axis_index("head")
    core, x, y = lax.rem(me, 2), lax.rem(me // 2, 4), me // 8
    half = y // 2
    other = 1 - half

    def device(yy, xx, cc):
        return (yy * 4 + xx) * 2 + cc

    y_pair = y + 1 - 2 * lax.rem(y, 2)
    ys = (y, 3 - y, y_pair, 3 - y_pair)
    right, left = lax.rem(x + 1, 4), lax.rem(x + 3, 4)
    partner = device(3 - y, x, core)
    targets = (device(y, right, core), device(y, left, core), device(y, x, 1 - core), device(y_pair, x, core))

    def remote(src, dst, ss, rs, ctx):
        return pltpu.make_async_remote_copy(
            src_ref=src, dst_ref=dst, send_sem=ss, recv_sem=rs, device_id={"ctx": ctx, "head": z}
        )

    barrier = pltpu.get_barrier_semaphore()

    @pl.loop(1, 32)
    def _(j):
        pl.semaphore_signal(barrier, inc=1, device_id={"ctx": lax.rem(me + j, 32), "head": z})

    for j in range(1, 4):
        pl.semaphore_signal(barrier, inc=1, device_id={"ctx": me, "head": lax.rem(z + j, 4)})
    mine_col = pl.multiple_of(half * HD, HD)
    other_col = pl.multiple_of(other * HD, HD)
    kv[0, core, 0] = k_soft[:, pl.ds(mine_col, HD)]
    kv[0, core, 1] = v_soft[:, pl.ds(mine_col, HD)]
    kv_out[0] = k_soft[:, pl.ds(other_col, HD)]
    kv_out[1] = v_soft[:, pl.ds(other_col, HD)]
    pl.semaphore_wait(barrier, 34)

    def hop(a, dx, kind):
        slot = 4 * a + dx
        if kind == 2:
            return remote(kv.at[slot, core], kv.at[slot, core], send.at[slot, 2], recv.at[slot, 2], targets[2])
        if kind == 3:
            to = 4 * (a + 2)
            return remote(kv.at[slot, core], kv.at[to, core], send.at[slot, 3], recv.at[to, 0], targets[3])
        if dx == 0:
            to = 4 * a + (3, 1)[kind]
            return remote(kv.at[slot, core], kv.at[to, core], send.at[slot, kind], recv.at[to, 0], targets[kind])
        to = 4 * a + 2
        part = pl.ds(128 * kind, 128)
        return remote(
            kv.at[slot, core, :, part], kv.at[to, core, :, part], send.at[slot, kind], recv.at[to, kind], targets[kind]
        )

    def kinds(a, dx):
        if dx == 0:
            return (3, 0, 1, 2) if a < 2 else (0, 1, 2)
        return {3: (0, 2), 1: (1, 2), 2: (2,)}[dx]

    swap_kv = remote(kv_out, kv.at[4, core], swap_send.at[0], swap_recv.at[0], partner)
    q_cols = pl.ds(pl.multiple_of(other * GROUP * HD, HD), GROUP * HD)
    swap_q = remote(q_soft.at[:, q_cols], q_in, swap_send.at[1], swap_recv.at[1], partner)

    def arrive(a, dx):
        slot = 4 * a + dx
        if (a, dx) == (1, 0):
            swap_kv.wait_recv()
        elif dx == 2:
            for kind in (0, 1):
                part = kv.at[slot, core, :, pl.ds(128 * kind, 128)]
                remote(part, part, send.at[slot, kind], recv.at[slot, kind], targets[2]).wait_recv()
        elif (a, dx) != (0, 0):
            part = kv.at[slot, core]
            remote(part, part, send.at[slot, 0], recv.at[slot, 0], targets[2]).wait_recv()
        for kind in kinds(a, dx):
            hop(a, dx, kind).start()

    arrive(0, 0)

    @pl.when(half == 0)
    def _():
        swap_kv.start()
        swap_q.start()

    @pl.when(half == 1)
    def _():
        swap_q.start()
        swap_kv.start()

    scale = math.log2(math.e) / math.sqrt(HD)

    def take_queries(g, ref, first):
        for r in range(GROUP):
            col = first + r * HD
            if not isinstance(col, int):
                col = pl.multiple_of(col, HD)
            high, low = halves(ref[:, pl.ds(col, HD)] * scale)
            rows = slice(r * ROWS, (r + 1) * ROWS)
            q3[g, rows, :HD] = high
            q3[g, rows, HD : 2 * HD] = high
            q3[g, rows, 2 * HD :] = low

    m_all[...] = jnp.full_like(m_all, NEGATIVE)
    l_all[...] = jnp.zeros_like(l_all)
    acc[...] = jnp.zeros_like(acc)

    rates = log_decay[...]
    s_at = lax.broadcasted_iota(jnp.int32, (ROWS, ROWS), 0)
    t_at = lax.broadcasted_iota(jnp.int32, (ROWS, ROWS), 1)
    cum_row[...] = jnp.dot(
        rates, jnp.where(s_at <= t_at, 1.0, 0.0), precision=lax.Precision.HIGHEST, preferred_element_type=F32
    )
    cum_col[...] = cum_row[...].T

    def lightning_head(hd):
        cols = slice(hd * HD, (hd + 1) * HD)
        q, k, v = q_lin[:, cols], k_lin[:, cols], v_lin[:, cols]
        down = cum_col[:, hd : hd + 1]
        gaps = jnp.where(t_at <= s_at, down - cum_row[hd : hd + 1, :], NEGATIVE)
        scores = dot3(q, k, NT)
        lin_out[:, cols] = dot3(scores * jnp.exp(gaps), v, (((1,), (0,)), ((), ())))
        total = cum_col[ROWS - 1 : ROWS, hd : hd + 1]
        state = dot3(k * jnp.exp(total - down), v, TN)
        for part in range(4):
            local[hd * 4 + part, :32] = state[part * 32 : (part + 1) * 32]
            local[hd * 4 + part, 32:] = jnp.broadcast_to(jnp.exp(total), (8, HD))

    for hd in range(4):
        lightning_head(hd)
    arrive(2, 0)
    for hd in range(4, 8):
        lightning_head(hd)

    def slice_out(j):
        to = lax.rem(me + j, 32)
        return remote(local.at[to], gathered.at[me], l_ss.at[j], l_rs.at[j], to)

    def slice_in(j):
        come = lax.rem(me + 32 - j, 32)
        return remote(local.at[me], gathered.at[come], l_ss.at[j], l_rs.at[j], come)

    @pl.loop(1, 32)
    def _(j):
        slice_out(j).start()

    gathered[me] = local[me]
    take_queries(0, q_soft, half * GROUP * HD)

    def prior_out(j):
        to = lax.rem(me + j, 32)
        return remote(prior.at[to], entering.at[me], e_ss.at[j], e_rs.at[j], to)

    def prior_in(j):
        come = lax.rem(me + 32 - j, 32)
        return remote(prior.at[me], entering.at[come], e_ss.at[j], e_rs.at[j], come)

    def combine():
        @pl.loop(1, 32)
        def _(j):
            slice_in(j).wait_recv()

        def turn(i, before):
            prior[i] = before
            return before * gathered[i, 32:33, :] + gathered[i, :32]

        lax.fori_loop(0, 32, turn, jnp.zeros((32, HD), F32))

        @pl.loop(1, 32)
        def _(j):
            prior_out(j).start()

        entering[me] = prior[me]

    def energy_out(j):
        return pltpu.make_async_remote_copy(
            src_ref=energy,
            dst_ref=energy_in.at[j - 1],
            send_sem=n_ss.at[j - 1],
            recv_sem=n_rs.at[j - 1],
            device_id={"ctx": me, "head": lax.rem(z + j, 4)},
        )

    def add_prior():
        @pl.loop(1, 32)
        def _(j):
            prior_in(j).wait_recv()

        sums = jnp.zeros((ROWS, HD), F32)
        for hd in range(8):
            cols = slice(hd * HD, (hd + 1) * HD)
            state = jnp.concatenate([entering[hd * 4 + part] for part in range(4)], 0)
            reach = dot3(q_lin[:, cols], state, (((1,), (0,)), ((), ())))
            linear = lin_out[:, cols] + jnp.exp(cum_col[:, hd : hd + 1]) * reach
            lin_out[:, cols] = linear
            sums = sums + linear * linear
        energy[...] = sums
        for j in range(1, 4):
            energy_out(j).start()

    def normalize():
        sums = energy[...]
        for j in range(1, 4):
            energy_out(j).wait_recv()
            sums = sums + energy_in[j - 1]
        total = jnp.sum(sums, axis=1, keepdims=True)
        ratio = jnp.broadcast_to(lax.rsqrt(total / (LH * HD) + EPSILON), (ROWS, HD))
        for hd in range(8):
            cols = slice(hd * HD, (hd + 1) * HD)
            lin_out[:, cols] = lin_out[:, cols] * ratio * gain[:, cols]

    def prepare(slot):
        part = kv.at[slot, 1 - core]
        remote(part, part, send.at[slot, 2], recv.at[slot, 2], targets[2]).wait_recv()
        for c in range(2):
            rows = slice(c * ROWS, (c + 1) * ROWS)
            high, low = halves(kv[slot, c, 0])
            k3[slot, rows, :HD] = high
            k3[slot, rows, HD : 2 * HD] = low
            k3[slot, rows, 2 * HD :] = high
            high, low = halves(kv[slot, c, 1])
            for copy in range(2):
                rows = slice(copy * KEYS + c * ROWS, copy * KEYS + (c + 1) * ROWS)
                v2[slot, rows, :HD] = high
                v2[slot, rows, HD:] = low

    def tile(g, slot, r, masked):
        rows = slice(r * ROWS, (r + 1) * ROWS)
        scores = lax.dot_general(q3[g, rows, :], k3[slot], NT, preferred_element_type=F32)
        if masked:
            at = lax.broadcasted_iota(jnp.int32, (ROWS, KEYS), 0) + core * ROWS
            key = lax.broadcasted_iota(jnp.int32, (ROWS, KEYS), 1)
            scores = jnp.where(key <= at, scores, NEGATIVE)
        before = m_all[g, rows, :]
        after = jnp.maximum(before, jnp.max(scores, axis=1, keepdims=True))
        weights = jnp.exp2(scores - jnp.concatenate([after] * (KEYS // HD), 1))
        shrink = jnp.exp2(before - after)
        sums = weights[:, :HD]
        for j in range(1, KEYS // HD):
            sums = sums + weights[:, j * HD : (j + 1) * HD]
        l_all[g, rows, :] = l_all[g, rows, :] * shrink + sums
        high, low = halves(weights)
        summed = jnp.dot(jnp.concatenate([high, low], 1), v2[slot], preferred_element_type=F32)
        acc[g, rows, :] = acc[g, rows, :] * jnp.concatenate([shrink, shrink], 1) + summed
        m_all[g, rows, :] = after

    def result(g, r):
        rows = slice(r * ROWS, (r + 1) * ROWS)
        total = jnp.sum(l_all[g, rows, :], axis=1, keepdims=True)
        return (acc[g, rows, :HD] + acc[g, rows, HD:]) / total

    def o_out(r, col):
        cols = pl.ds(pl.multiple_of(col * GROUP * HD + r * HD, HD), HD)
        return remote(o_send.at[r], soft_out.at[:, cols], o_ss.at[r], o_rs.at[r], partner)

    events = {
        0: lambda: (arrive(0, 3), arrive(0, 1)),
        1: lambda: (arrive(2, 3), arrive(2, 1), combine()),
        2: lambda: arrive(0, 2),
        3: lambda: arrive(2, 2),
        4: lambda: arrive(1, 0),
        5: lambda: arrive(3, 0),
        8: lambda: (swap_q.wait_recv(), take_queries(1, q_in, 0), add_prior()),
        9: lambda: (arrive(1, 3), arrive(1, 1)),
        10: lambda: (arrive(3, 3), arrive(3, 1)),
        12: lambda: arrive(1, 2),
        13: lambda: arrive(3, 2),
        14: normalize,
    }
    mine_at, partner_at = y * 4 + x, (3 - y) * 4 + x

    def pick(k, values):
        out = values[0]
        for at in range(1, 8):
            out = jnp.where(k == at, values[at], out)
        return out

    @pl.loop(0, 32)
    def _(t):
        for at, act in events.items():

            @pl.when(t == at)
            def _(act=act):
                act()

        k = lax.rem(t, 8)
        far = t // 16
        g = jnp.where((t >= 8) & (t < 24), 1, 0)
        a = pick(k, [p[0] for p in NEAR]) + far
        dx = pick(k, [p[1] for p in NEAR])
        slot = 4 * a + dx
        row = jnp.where(a == 0, ys[0], jnp.where(a == 1, ys[1], jnp.where(a == 2, ys[2], ys[3])))
        keys_at = row * 4 + lax.rem(x + dx, 4)
        asks = jnp.where(g == 0, mine_at, partner_at)

        @pl.when((t < 8) | ((t >= 16) & (t < 24)))
        def _():
            prepare(slot)

        @pl.when(keys_at < asks)
        def _():
            for r in range(GROUP):
                tile(g, slot, r, False)

        @pl.when(keys_at == asks)
        def _():
            for r in range(GROUP):
                tile(g, slot, r, True)

        @pl.when(t == 23)
        def _():
            for r in range(GROUP):
                o_send[r] = result(1, r)
                o_out(r, half).start()

    for r in range(GROUP):
        cols = pl.ds(pl.multiple_of(half * GROUP * HD + r * HD, HD), HD)
        soft_out[:, cols] = result(0, r)
    for r in range(GROUP):
        o_out(r, other).wait_recv()

    swap_kv.wait_send()
    swap_q.wait_send()
    for a in range(4):
        for dx in range(4):
            for kind in kinds(a, dx):
                hop(a, dx, kind).wait_send()
    for r in range(GROUP):
        o_out(r, half).wait_send()
    for j in range(1, 4):
        energy_out(j).wait_send()

    @pl.loop(1, 32)
    def _(j):
        slice_out(j).wait_send()
        prior_out(j).wait_send()


def body(q_lin, k_lin, v_lin, log_decay, lin_gain, q_soft, k_soft, v_soft):
    vmem = pl.BlockSpec(memory_space=pltpu.VMEM)
    dma = pltpu.SemaphoreType.DMA
    return pl.pallas_call(
        kernel,
        out_shape=(
            jax.ShapeDtypeStruct(q_lin.shape, F32),
            jax.ShapeDtypeStruct(q_soft.shape, F32),
        ),
        in_specs=[vmem] * 8,
        out_specs=(vmem, vmem),
        scratch_shapes=[
            pltpu.VMEM((16, 2, 2, ROWS, HD), F32),
            pltpu.VMEM((2, ROWS, HD), F32),
            pltpu.VMEM((ROWS, GROUP * HD), F32),
            pltpu.VMEM((2, TILES, 3 * HD), BF16),
            pltpu.VMEM((16, KEYS, 3 * HD), BF16),
            pltpu.VMEM((16, 2 * KEYS, 2 * HD), BF16),
            pltpu.VMEM((2, TILES, HD), F32),
            pltpu.VMEM((2, TILES, HD), F32),
            pltpu.VMEM((2, TILES, 2 * HD), F32),
            pltpu.VMEM((GROUP, ROWS, HD), F32),
            pltpu.VMEM((32, 40, HD), F32),
            pltpu.VMEM((32, 40, HD), F32),
            pltpu.VMEM((32, 32, HD), F32),
            pltpu.VMEM((32, 32, HD), F32),
            pltpu.VMEM((ROWS, HD), F32),
            pltpu.VMEM((3, ROWS, HD), F32),
            pltpu.VMEM((8, ROWS), F32),
            pltpu.VMEM((ROWS, 8), F32),
            dma((2,)), dma((2,)), dma((16, 4)), dma((16, 3)), dma((GROUP,)), dma((GROUP,)),
            dma((32,)), dma((32,)), dma((32,)), dma((32,)), dma((3,)), dma((3,)),
        ],
        compiler_params=pltpu.CompilerParams(
            collective_id=0, has_side_effects=True, vmem_limit_bytes=60 << 20
        ),
        cost_estimate=pl.CostEstimate(
            flops=34 * 4 * TILES * ROWS * HD, bytes_accessed=12 << 20, transcendentals=34 * TILES * ROWS
        ),
        name="attention",
    )(q_lin, k_lin, v_lin, log_decay, lin_gain.reshape(1, -1), q_soft, k_soft, v_soft)


def solution(mesh):
    return jax.shard_map(
        body,
        mesh=mesh,
        in_specs=(
            P("ctx", "head"),
            P("ctx", "head"),
            P("ctx", "head"),
            P("head", "ctx"),
            P("head"),
            P("ctx", "head"),
            P("ctx", "head"),
            P("ctx", "head"),
        ),
        out_specs=(P("ctx", "head"), P("ctx", "head")),
        check_vma=False,
    )
```

```python
import functools
import math

import jax
import jax.numpy as jnp
from jax import lax
from jax.experimental import pallas as pl
from jax.experimental.pallas import tpu as pltpu
from jax.sharding import PartitionSpec as P

HD = 128
LH = 32
EPSILON = 1e-05
NEGATIVE = -1e30
F32 = jnp.float32
BF16 = jnp.bfloat16
NT = (((1,), (1,)), ((), ()))
TN = (((0,), (0,)), ((), ()))
ROWS = 256
KEYS = 512
GROUP = 6
TILES = GROUP * ROWS
COLUMNS = (0, 3, 1, 2)
LOW = ((0, 0, 1), (1, 0, 0), (0, 2, 1), (1, 2, 0), (1, 1, 1), (1, 3, 1))
HIGH = ((0, 0, 1), (0, 1, 1), (1, 1, 0), (1, 3, 1), (0, 3, 0), (0, 2, 1))


def halves(value):
    high = value.astype(BF16)
    return high, (value - high.astype(F32)).astype(BF16)


def dot3(left, right, dims):
    (la,), (ra,) = dims[0]
    lh, ll = halves(left)
    rh, rl = halves(right)
    return lax.dot_general(
        jnp.concatenate([lh, ll, lh], la),
        jnp.concatenate([rh, rh, rl], ra),
        dims,
        preferred_element_type=F32,
    )


def kernel(
    q_lin, k_lin, v_lin, log_decay, gain, q_soft, k_soft, v_soft,
    lin_out, soft_out,
    kv, kv_out, q_in, q3, k3, v2, m_all, l_all, acc, o_send,
    local, gathered, prior, reach_decay, row_out, row_in, entering, energy, energy_in, cum_row, cum_col,
    swap_send, swap_recv, send, recv, o_ss, o_rs, l_ss, l_rs, r_ss, r_rs, e_ss, e_rs, n_ss, n_rs,
):
    me = lax.axis_index("ctx")
    z = lax.axis_index("head")
    core, x, y = lax.rem(me, 2), lax.rem(me // 2, 4), me // 8
    half = y // 2
    other = 1 - half
    low, high_half = half == 0, half == 1
    inner = (y == 1) | (y == 2)
    always = y >= 0

    def device(yy, xx, cc):
        return (yy * 4 + xx) * 2 + cc

    y_pair = y + 1 - 2 * lax.rem(y, 2)
    ys = (y, 3 - y, y_pair, 3 - y_pair)
    right, left = lax.rem(x + 1, 4), lax.rem(x + 3, 4)
    partner = device(3 - y, x, core)
    across = lax.rem(x + 2, 4)
    targets = (
        device(y, right, core),
        device(y, left, core),
        device(y, x, 1 - core),
        device(y_pair, x, core),
        device(y, across, core),
    )

    def remote(src, dst, ss, rs, ctx):
        return pltpu.make_async_remote_copy(
            src_ref=src, dst_ref=dst, send_sem=ss, recv_sem=rs, device_id={"ctx": ctx, "head": z}
        )

    barrier = pltpu.get_barrier_semaphore()

    at_row = lax.rem(me, 8)
    row_start = me - at_row

    @pl.loop(1, 8)
    def _(j):
        pl.semaphore_signal(barrier, inc=1, device_id={"ctx": row_start + lax.rem(at_row + j, 8), "head": z})

    @pl.loop(1, 4)
    def _(j):
        pl.semaphore_signal(barrier, inc=1, device_id={"ctx": device(lax.rem(y + j, 4), x, core), "head": z})

    for j in range(1, 4):
        pl.semaphore_signal(barrier, inc=1, device_id={"ctx": me, "head": lax.rem(z + j, 4)})
    mine_col = pl.multiple_of(half * HD, HD)
    other_col = pl.multiple_of(other * HD, HD)
    kv[0, core, 0] = k_soft[:, pl.ds(mine_col, HD)]
    kv[0, core, 1] = v_soft[:, pl.ds(mine_col, HD)]
    kv_out[0] = k_soft[:, pl.ds(other_col, HD)]
    kv_out[1] = v_soft[:, pl.ds(other_col, HD)]
    pl.semaphore_wait(barrier, 13)

    def hop(a, dx, kind):
        slot = 4 * a + dx
        to = {0: 4 * a + 3, 1: 4 * a + 1, 4: 4 * a + 2, 2: slot, 3: slot + 8}[kind]
        return remote(
            kv.at[slot, core], kv.at[to, core], send.at[slot, kind], recv.at[to, int(kind == 2)], targets[kind]
        )

    def present(a):
        return (always, always, jnp.logical_not(inner & high_half), jnp.logical_not(inner & low))[a]

    def onward(a, dx):
        out = []
        if a < 2:
            out.append((inner | (low, high_half)[a] if dx == 0 else inner, 3))
            if a == 1 and dx != 0:
                out = []
        if dx == 0:
            when = (always, always, inner & low, present(3))[a]
            out += [(when, 0), (when, 1), (when, 4)]
        return out + [(present(a), 2)]

    swap_kv = remote(kv_out, kv.at[4, core], swap_send.at[0], swap_recv.at[0], partner)
    q_cols = pl.ds(pl.multiple_of(other * GROUP * HD, HD), GROUP * HD)
    swap_q = remote(q_soft.at[:, q_cols], q_in, swap_send.at[1], swap_recv.at[1], partner)

    def guarded(when, act):
        if when is always:
            act()
        else:
            pl.when(when)(act)

    def arrive(a, dx):
        slot = 4 * a + dx

        def wait():
            part = kv.at[slot, core]
            remote(part, part, send.at[slot, 0], recv.at[slot, 0], targets[2]).wait_recv()

        if (a, dx) == (1, 0):
            swap_kv.wait_recv()
        elif (a, dx) != (0, 0):
            guarded(present(a), wait)
        for when, kind in onward(a, dx):
            guarded(when, lambda kind=kind: hop(a, dx, kind).start())

    arrive(0, 0)

    @pl.when(half == 0)
    def _():
        swap_kv.start()
        swap_q.start()

    @pl.when(half == 1)
    def _():
        swap_q.start()
        swap_kv.start()

    scale = math.log2(math.e) / math.sqrt(HD)

    def take_queries(g, ref, first):
        for r in range(GROUP):
            col = first + r * HD
            if not isinstance(col, int):
                col = pl.multiple_of(col, HD)
            high, low = halves(ref[:, pl.ds(col, HD)] * scale)
            rows = slice(r * ROWS, (r + 1) * ROWS)
            q3[g, rows, :HD] = high
            q3[g, rows, HD : 2 * HD] = high
            q3[g, rows, 2 * HD :] = low

    m_all[...] = jnp.full_like(m_all, NEGATIVE)
    l_all[...] = jnp.zeros_like(l_all)
    acc[...] = jnp.zeros_like(acc)

    rates = log_decay[...]
    s_at = lax.broadcasted_iota(jnp.int32, (ROWS, ROWS), 0)
    t_at = lax.broadcasted_iota(jnp.int32, (ROWS, ROWS), 1)
    cum_row[...] = jnp.dot(
        rates, jnp.where(s_at <= t_at, 1.0, 0.0), precision=lax.Precision.HIGHEST, preferred_element_type=F32
    )
    cum_col[...] = cum_row[...].T

    def lightning_head(hd):
        cols = slice(hd * HD, (hd + 1) * HD)
        q, k, v = q_lin[:, cols], k_lin[:, cols], v_lin[:, cols]
        down = cum_col[:, hd : hd + 1]
        gaps = jnp.where(t_at <= s_at, down - cum_row[hd : hd + 1, :], NEGATIVE)
        scores = dot3(q, k, NT)
        lin_out[:, cols] = dot3(scores * jnp.exp(gaps), v, (((1,), (0,)), ((), ())))
        total = cum_col[ROWS - 1 : ROWS, hd : hd + 1]
        state = dot3(k * jnp.exp(total - down), v, TN)
        local[hd, :HD] = state
        local[hd, HD:] = jnp.broadcast_to(jnp.exp(total), (8, HD))

    for hd in range(8):
        lightning_head(hd)

    def slice_out(j):
        to = lax.rem(at_row + j, 8)
        return remote(local.at[to], gathered.at[at_row], l_ss.at[j], l_rs.at[j], row_start + to)

    def slice_in(j):
        come = lax.rem(at_row + 8 - j, 8)
        return remote(local.at[at_row], gathered.at[come], l_ss.at[j], l_rs.at[j], row_start + come)

    @pl.loop(1, 8)
    def _(j):
        slice_out(j).start()

    gathered[at_row] = local[at_row]
    take_queries(0, q_soft, half * GROUP * HD)

    def total_out(j):
        return remote(row_out, row_in.at[y], r_ss.at[j], r_rs.at[j], device(lax.rem(y + j, 4), x, core))

    def total_in(j):
        come = lax.rem(y + 4 - j, 4)
        return remote(row_out, row_in.at[come], r_ss.at[j], r_rs.at[j], device(come, x, core))

    def combine_row():
        @pl.loop(1, 8)
        def _(j):
            slice_in(j).wait_recv()

        decay = jnp.ones((8, HD), F32)
        state = jnp.zeros((HD, HD), F32)
        for i in range(8):
            prior[i] = state
            reach_decay[i] = decay
            state = state * gathered[i, HD : HD + 1, :] + gathered[i, :HD]
            decay = decay * gathered[i, HD:, :]
        row_out[:HD] = state
        row_out[HD:] = decay

        @pl.loop(1, 4)
        def _(j):
            total_out(j).start()

    def prior_out(j):
        to = lax.rem(at_row + j, 8)
        return remote(prior.at[to], entering.at[at_row], e_ss.at[j], e_rs.at[j], row_start + to)

    def prior_in(j):
        come = lax.rem(at_row + 8 - j, 8)
        return remote(prior.at[at_row], entering.at[come], e_ss.at[j], e_rs.at[j], row_start + come)

    def combine():
        @pl.loop(1, 4)
        def _(j):
            total_in(j).wait_recv()

        row_in[y] = row_out[...]
        state = jnp.zeros((HD, HD), F32)
        for i in range(3):
            state = jnp.where(i < y, state * row_in[i, HD : HD + 1, :] + row_in[i, :HD], state)
        for i in range(8):
            prior[i] = prior[i] + reach_decay[i, :1, :] * state

        @pl.loop(1, 8)
        def _(j):
            prior_out(j).start()

        entering[at_row] = prior[at_row]

    def energy_out(j):
        return pltpu.make_async_remote_copy(
            src_ref=energy,
            dst_ref=energy_in.at[j - 1],
            send_sem=n_ss.at[j - 1],
            recv_sem=n_rs.at[j - 1],
            device_id={"ctx": me, "head": lax.rem(z + j, 4)},
        )

    def add_prior():
        @pl.loop(1, 8)
        def _(j):
            prior_in(j).wait_recv()

        sums = jnp.zeros((ROWS, HD), F32)
        for hd in range(8):
            cols = slice(hd * HD, (hd + 1) * HD)
            reach = dot3(q_lin[:, cols], entering[hd], (((1,), (0,)), ((), ())))
            linear = lin_out[:, cols] + jnp.exp(cum_col[:, hd : hd + 1]) * reach
            lin_out[:, cols] = linear
            sums = sums + linear * linear
        energy[...] = sums
        for j in range(1, 4):
            energy_out(j).start()

    def normalize():
        sums = energy[...]
        for j in range(1, 4):
            energy_out(j).wait_recv()
            sums = sums + energy_in[j - 1]
        total = jnp.sum(sums, axis=1, keepdims=True)
        ratio = jnp.broadcast_to(lax.rsqrt(total / (LH * HD) + EPSILON), (ROWS, HD))
        for hd in range(8):
            cols = slice(hd * HD, (hd + 1) * HD)
            lin_out[:, cols] = lin_out[:, cols] * ratio * gain[:, cols]

    def prepare(slot):
        part = kv.at[slot, 1 - core]
        remote(part, part, send.at[slot, 2], recv.at[slot, 1], targets[2]).wait_recv()
        for c in range(2):
            rows = slice(c * ROWS, (c + 1) * ROWS)
            high, low = halves(kv[slot, c, 0])
            k3[slot, rows, :HD] = high
            k3[slot, rows, HD : 2 * HD] = low
            k3[slot, rows, 2 * HD :] = high
            high, low = halves(kv[slot, c, 1])
            for copy in range(2):
                rows = slice(copy * KEYS + c * ROWS, copy * KEYS + (c + 1) * ROWS)
                v2[slot, rows, :HD] = high
                v2[slot, rows, HD:] = low

    def tile(g, slot, r, masked):
        rows = slice(r * ROWS, (r + 1) * ROWS)
        scores = lax.dot_general(q3[g, rows, :], k3[slot], NT, preferred_element_type=F32)
        if masked:
            at = lax.broadcasted_iota(jnp.int32, (ROWS, KEYS), 0) + core * ROWS
            key = lax.broadcasted_iota(jnp.int32, (ROWS, KEYS), 1)
            scores = jnp.where(key <= at, scores, NEGATIVE)
        before = m_all[g, rows, :]
        after = jnp.maximum(before, jnp.max(scores, axis=1, keepdims=True))
        weights = jnp.exp2(scores - jnp.concatenate([after] * (KEYS // HD), 1))
        shrink = jnp.exp2(before - after)
        sums = weights[:, :HD]
        for j in range(1, KEYS // HD):
            sums = sums + weights[:, j * HD : (j + 1) * HD]
        l_all[g, rows, :] = l_all[g, rows, :] * shrink + sums
        high, low = halves(weights)
        summed = jnp.dot(jnp.concatenate([high, low], 1), v2[slot], preferred_element_type=F32)
        acc[g, rows, :] = acc[g, rows, :] * jnp.concatenate([shrink, shrink], 1) + summed
        m_all[g, rows, :] = after

    def result(g, r):
        rows = slice(r * ROWS, (r + 1) * ROWS)
        total = jnp.sum(l_all[g, rows, :], axis=1, keepdims=True)
        return (acc[g, rows, :HD] + acc[g, rows, HD:]) / total

    def o_out(r, col):
        cols = pl.ds(pl.multiple_of(col * GROUP * HD + r * HD, HD), HD)
        return remote(o_send.at[r], soft_out.at[:, cols], o_ss.at[r], o_rs.at[r], partner)

    def take_partner():
        swap_q.wait_recv()
        take_queries(1, q_in, 0)

    def give_back():
        for r in range(GROUP):
            o_send[r] = result(1, r)
            o_out(r, half).start()

    def column(a):
        for dx in (3, 1, 2):
            arrive(a, dx)

    events = (
        (0, 10, lambda: arrive(2, 0)),
        (6, 0, lambda: arrive(1, 0)),
        (1, 1, lambda: column(0)),
        (2, 2, combine_row),
        (8, 3, lambda: arrive(3, 0)),
        (4, 4, combine),
        (16, 4, lambda: column(1)),
        (4, 8, take_partner),
        (8, 8, add_prior),
        (9, 20, lambda: column(2)),
        (12, 12, normalize),
        (20, 12, lambda: column(3)),
        (24, 16, give_back),
    )
    mine_at, partner_at = y * 4 + x, (3 - y) * 4 + x

    def pick(k, values):
        out = values[0]
        for at in range(1, len(values)):
            out = jnp.where(k == at, values[at], out)
        return out

    def table(k, column):
        return jnp.where(low, pick(k, [s[column] for s in LOW]), pick(k, [s[column] for s in HIGH]))

    @pl.loop(0, 25)
    def _(t):
        for at_low, at_high, act in events:
            pl.when(t == jnp.where(low, at_low, at_high))(act)

        k = lax.rem(t, 4)
        step = t // 4
        g, a = table(step, 0), table(step, 1)
        dx = pick(k, COLUMNS)
        slot = 4 * a + dx
        row = pick(a, ys)
        keys_at = row * 4 + lax.rem(x + dx, 4)
        asks = jnp.where(t == 24, -1, jnp.where(g == 0, mine_at, partner_at))
        here = pick(a, [present(p).astype(jnp.int32) for p in range(4)])

        @pl.when((table(step, 2) == 1) & (t < 24) & (here == 1))
        def _():
            prepare(slot)

        @pl.when(keys_at < asks)
        def _():
            for r in range(GROUP):
                tile(g, slot, r, False)

        @pl.when(keys_at == asks)
        def _():
            for r in range(GROUP):
                tile(g, slot, r, True)

    for r in range(GROUP):
        cols = pl.ds(pl.multiple_of(half * GROUP * HD + r * HD, HD), HD)
        soft_out[:, cols] = result(0, r)
    for r in range(GROUP):
        o_out(r, other).wait_recv()

    swap_kv.wait_send()
    swap_q.wait_send()
    for a in range(4):
        for dx in range(4):
            for when, kind in onward(a, dx):
                guarded(when, lambda a=a, dx=dx, kind=kind: hop(a, dx, kind).wait_send())
    for r in range(GROUP):
        o_out(r, half).wait_send()
    for j in range(1, 4):
        energy_out(j).wait_send()

    @pl.loop(1, 8)
    def _(j):
        slice_out(j).wait_send()
        prior_out(j).wait_send()

    @pl.loop(1, 4)
    def _(j):
        total_out(j).wait_send()


def body(q_lin, k_lin, v_lin, log_decay, lin_gain, q_soft, k_soft, v_soft):
    vmem = pl.BlockSpec(memory_space=pltpu.VMEM)
    dma = pltpu.SemaphoreType.DMA
    return pl.pallas_call(
        kernel,
        out_shape=(
            jax.ShapeDtypeStruct(q_lin.shape, F32),
            jax.ShapeDtypeStruct(q_soft.shape, F32),
        ),
        in_specs=[vmem] * 8,
        out_specs=(vmem, vmem),
        scratch_shapes=[
            pltpu.VMEM((16, 2, 2, ROWS, HD), F32),
            pltpu.VMEM((2, ROWS, HD), F32),
            pltpu.VMEM((ROWS, GROUP * HD), F32),
            pltpu.VMEM((2, TILES, 3 * HD), BF16),
            pltpu.VMEM((16, KEYS, 3 * HD), BF16),
            pltpu.VMEM((16, 2 * KEYS, 2 * HD), BF16),
            pltpu.VMEM((2, TILES, HD), F32),
            pltpu.VMEM((2, TILES, HD), F32),
            pltpu.VMEM((2, TILES, 2 * HD), F32),
            pltpu.VMEM((GROUP, ROWS, HD), F32),
            pltpu.VMEM((8, HD + 8, HD), F32),
            pltpu.VMEM((8, HD + 8, HD), F32),
            pltpu.VMEM((8, HD, HD), F32),
            pltpu.VMEM((8, 8, HD), F32),
            pltpu.VMEM((HD + 8, HD), F32),
            pltpu.VMEM((4, HD + 8, HD), F32),
            pltpu.VMEM((8, HD, HD), F32),
            pltpu.VMEM((ROWS, HD), F32),
            pltpu.VMEM((3, ROWS, HD), F32),
            pltpu.VMEM((8, ROWS), F32),
            pltpu.VMEM((ROWS, 8), F32),
            dma((2,)), dma((2,)), dma((16, 5)), dma((16, 2)), dma((GROUP,)), dma((GROUP,)),
            dma((8,)), dma((8,)), dma((4,)), dma((4,)), dma((8,)), dma((8,)), dma((3,)), dma((3,)),
        ],
        compiler_params=pltpu.CompilerParams(
            collective_id=0, has_side_effects=True, vmem_limit_bytes=60 << 20
        ),
        cost_estimate=pl.CostEstimate(
            flops=34 * 4 * TILES * ROWS * HD, bytes_accessed=12 << 20, transcendentals=34 * TILES * ROWS
        ),
        name="attention",
    )(q_lin, k_lin, v_lin, log_decay, lin_gain.reshape(1, -1), q_soft, k_soft, v_soft)


def solution(mesh):
    return jax.shard_map(
        body,
        mesh=mesh,
        in_specs=(
            P("ctx", "head"),
            P("ctx", "head"),
            P("ctx", "head"),
            P("head", "ctx"),
            P("head"),
            P("ctx", "head"),
            P("ctx", "head"),
            P("ctx", "head"),
        ),
        out_specs=(P("ctx", "head"), P("ctx", "head")),
        check_vma=False,
    )
```

```python
import functools
import math

import jax
import jax.numpy as jnp
from jax import lax
from jax.experimental import pallas as pl
from jax.experimental.pallas import tpu as pltpu
from jax.sharding import PartitionSpec as P

HD = 128
LH = 32
EPSILON = 1e-05
NEGATIVE = -1e30
F32 = jnp.float32
BF16 = jnp.bfloat16
NT = (((1,), (1,)), ((), ()))
TN = (((0,), (0,)), ((), ()))
ROWS = 256
KEYS = 512
GROUP = 6
TILES = GROUP * ROWS
COLUMNS = (0, 3, 1, 2)
LOW = ((0, 0, 1), (1, 0, 0), (0, 2, 1), (1, 2, 0), (0, 0, 0), (0, 0, 0))
HIGH = ((0, 0, 1), (0, 1, 1), (1, 1, 0), (1, 3, 1), (0, 3, 0), (0, 2, 1))


def halves(value):
    high = value.astype(BF16)
    return high, (value - high.astype(F32)).astype(BF16)


def dot3(left, right, dims):
    (la,), (ra,) = dims[0]
    lh, ll = halves(left)
    rh, rl = halves(right)
    return lax.dot_general(
        jnp.concatenate([lh, ll, lh], la),
        jnp.concatenate([rh, rh, rl], ra),
        dims,
        preferred_element_type=F32,
    )


def kernel(
    q_lin_all, k_lin_all, v_lin_all, log_decay, gain, q_soft, k_soft, v_soft,
    lin_out, soft_out,
    q_lin, k_lin, v_lin, kv, q_own, q_in, q3, k3, v2, m_all, l_all, acc, o_send,
    local, gathered, prior, reach_decay, row_out, row_in, entering, energy, energy_in, cum_row, cum_col,
    loaded, swap_send, swap_recv, send, recv, o_ss, o_rs, l_ss, l_rs, r_ss, r_rs, e_ss, e_rs, n_ss, n_rs,
):
    me = lax.axis_index("ctx")
    z = lax.axis_index("head")
    core, x, y = lax.rem(me, 2), lax.rem(me // 2, 4), me // 8
    half = y // 2
    other = 1 - half
    low, high_half = half == 0, half == 1
    inner = (y == 1) | (y == 2)
    always = y >= 0

    def device(yy, xx, cc):
        return (yy * 4 + xx) * 2 + cc

    y_pair = y + 1 - 2 * lax.rem(y, 2)
    ys = (y, 3 - y, y_pair, 3 - y_pair)
    right, left = lax.rem(x + 1, 4), lax.rem(x + 3, 4)
    partner = device(3 - y, x, core)
    across = lax.rem(x + 2, 4)
    targets = (
        device(y, right, core),
        device(y, left, core),
        device(y, x, 1 - core),
        device(y_pair, x, core),
        device(y, across, core),
    )

    def remote(src, dst, ss, rs, ctx):
        return pltpu.make_async_remote_copy(
            src_ref=src, dst_ref=dst, send_sem=ss, recv_sem=rs, device_id={"ctx": ctx, "head": z}
        )

    barrier = pltpu.get_barrier_semaphore()

    at_row = lax.rem(me, 8)
    row_start = me - at_row

    @pl.loop(1, 8)
    def _(j):
        pl.semaphore_signal(barrier, inc=1, device_id={"ctx": row_start + lax.rem(at_row + j, 8), "head": z})

    @pl.loop(1, 4)
    def _(j):
        pl.semaphore_signal(barrier, inc=1, device_id={"ctx": device(lax.rem(y + j, 4), x, core), "head": z})

    for j in range(1, 4):
        pl.semaphore_signal(barrier, inc=1, device_id={"ctx": me, "head": lax.rem(z + j, 4)})
    mine = pl.ds(pl.multiple_of(half * HD, HD), HD)
    others = pl.ds(pl.multiple_of(other * HD, HD), HD)
    loads = [
        pltpu.make_async_copy(k_soft.at[:, mine], kv.at[0, core, 0], loaded.at[0]),
        pltpu.make_async_copy(v_soft.at[:, mine], kv.at[0, core, 1], loaded.at[1]),
        pltpu.make_async_copy(q_lin_all, q_lin, loaded.at[2]),
        pltpu.make_async_copy(k_lin_all, k_lin, loaded.at[3]),
        pltpu.make_async_copy(v_lin_all, v_lin, loaded.at[4]),
        pltpu.make_async_copy(
            q_soft.at[:, pl.ds(pl.multiple_of(half * GROUP * HD, HD), GROUP * HD)], q_own, loaded.at[5]
        ),
    ]
    for load in loads:
        load.start()
    pl.semaphore_wait(barrier, 13)

    def hop(a, dx, kind):
        slot = 4 * a + dx
        to = {0: 4 * a + 3, 1: 4 * a + 1, 4: 4 * a + 2, 2: slot, 3: slot + 8}[kind]
        return remote(
            kv.at[slot, core], kv.at[to, core], send.at[slot, kind], recv.at[to, int(kind == 2)], targets[kind]
        )

    def present(a):
        return (always, always, jnp.logical_not(inner & high_half), jnp.logical_not(inner & low))[a]

    def onward(a, dx):
        out = []
        if a < 2:
            out.append((inner | (low, high_half)[a] if dx == 0 else inner, 3))
            if a == 1 and dx != 0:
                out = []
        if dx == 0:
            when = (always, always, inner & low, present(3))[a]
            out += [(when, 0), (when, 1), (when, 4)]
        return out + [(present(a), 2)]

    swap_k = remote(k_soft.at[:, others], kv.at[4, core, 0], swap_send.at[0], swap_recv.at[0], partner)
    swap_v = remote(v_soft.at[:, others], kv.at[4, core, 1], swap_send.at[2], swap_recv.at[2], partner)
    q_cols = pl.ds(pl.multiple_of(other * GROUP * HD, HD), GROUP * HD)
    swap_q = remote(q_soft.at[:, q_cols], q_in, swap_send.at[1], swap_recv.at[1], partner)

    def guarded(when, act):
        if when is always:
            act()
        else:
            pl.when(when)(act)

    def arrive(a, dx):
        slot = 4 * a + dx

        def wait():
            part = kv.at[slot, core]
            remote(part, part, send.at[slot, 0], recv.at[slot, 0], targets[2]).wait_recv()

        if (a, dx) == (1, 0):
            swap_k.wait_recv()
            swap_v.wait_recv()
        elif (a, dx) != (0, 0):
            guarded(present(a), wait)
        for when, kind in onward(a, dx):
            guarded(when, lambda kind=kind: hop(a, dx, kind).start())

    @pl.when(low)
    def _():
        swap_k.start()
        swap_v.start()
        swap_q.start()

    @pl.when(high_half)
    def _():
        swap_q.start()
        swap_k.start()
        swap_v.start()

    loads[0].wait()
    loads[1].wait()
    arrive(0, 0)

    scale = math.log2(math.e) / math.sqrt(HD)

    def take_queries(g, ref):
        for r in range(GROUP):
            col = r * HD
            high, low = halves(ref[:, pl.ds(col, HD)] * scale)
            rows = slice(r * ROWS, (r + 1) * ROWS)
            q3[g, rows, :HD] = high
            q3[g, rows, HD : 2 * HD] = high
            q3[g, rows, 2 * HD :] = low

    m_all[...] = jnp.full_like(m_all, NEGATIVE)
    l_all[...] = jnp.zeros_like(l_all)
    acc[...] = jnp.zeros_like(acc)

    rates = log_decay[...]
    s_at = lax.broadcasted_iota(jnp.int32, (ROWS, ROWS), 0)
    t_at = lax.broadcasted_iota(jnp.int32, (ROWS, ROWS), 1)
    cum_row[...] = jnp.dot(
        rates, jnp.where(s_at <= t_at, 1.0, 0.0), precision=lax.Precision.HIGHEST, preferred_element_type=F32
    )
    cum_col[...] = cum_row[...].T

    def lightning_head(hd):
        cols = slice(hd * HD, (hd + 1) * HD)
        q, k, v = q_lin[:, cols], k_lin[:, cols], v_lin[:, cols]
        down = cum_col[:, hd : hd + 1]
        gaps = jnp.where(t_at <= s_at, down - cum_row[hd : hd + 1, :], NEGATIVE)
        scores = dot3(q, k, NT)
        lin_out[:, cols] = dot3(scores * jnp.exp(gaps), v, (((1,), (0,)), ((), ())))
        total = cum_col[ROWS - 1 : ROWS, hd : hd + 1]
        state = dot3(k * jnp.exp(total - down), v, TN)
        local[hd, :HD] = state
        local[hd, HD:] = jnp.broadcast_to(jnp.exp(total), (8, HD))

    for at in (2, 3, 4):
        loads[at].wait()
    for hd in range(8):
        lightning_head(hd)

    def slice_out(j):
        to = lax.rem(at_row + j, 8)
        return remote(local.at[to], gathered.at[at_row], l_ss.at[j], l_rs.at[j], row_start + to)

    def slice_in(j):
        come = lax.rem(at_row + 8 - j, 8)
        return remote(local.at[at_row], gathered.at[come], l_ss.at[j], l_rs.at[j], row_start + come)

    @pl.loop(1, 8)
    def _(j):
        slice_out(j).start()

    gathered[at_row] = local[at_row]
    loads[5].wait()
    take_queries(0, q_own)

    def total_out(j):
        return remote(row_out, row_in.at[y], r_ss.at[j], r_rs.at[j], device(lax.rem(y + j, 4), x, core))

    def total_in(j):
        come = lax.rem(y + 4 - j, 4)
        return remote(row_out, row_in.at[come], r_ss.at[j], r_rs.at[j], device(come, x, core))

    def combine_row():
        @pl.loop(1, 8)
        def _(j):
            slice_in(j).wait_recv()

        decay = jnp.ones((8, HD), F32)
        state = jnp.zeros((HD, HD), F32)
        for i in range(8):
            prior[i] = state
            reach_decay[i] = decay
            state = state * gathered[i, HD : HD + 1, :] + gathered[i, :HD]
            decay = decay * gathered[i, HD:, :]
        row_out[:HD] = state
        row_out[HD:] = decay

        @pl.loop(1, 4)
        def _(j):
            total_out(j).start()

    def prior_out(j):
        to = lax.rem(at_row + j, 8)
        return remote(prior.at[to], entering.at[at_row], e_ss.at[j], e_rs.at[j], row_start + to)

    def prior_in(j):
        come = lax.rem(at_row + 8 - j, 8)
        return remote(prior.at[at_row], entering.at[come], e_ss.at[j], e_rs.at[j], row_start + come)

    def combine():
        @pl.loop(1, 4)
        def _(j):
            total_in(j).wait_recv()

        row_in[y] = row_out[...]
        state = jnp.zeros((HD, HD), F32)
        for i in range(3):
            state = jnp.where(i < y, state * row_in[i, HD : HD + 1, :] + row_in[i, :HD], state)
        for i in range(8):
            prior[i] = prior[i] + reach_decay[i, :1, :] * state

        @pl.loop(1, 8)
        def _(j):
            prior_out(j).start()

        entering[at_row] = prior[at_row]

    def energy_out(j):
        return pltpu.make_async_remote_copy(
            src_ref=energy,
            dst_ref=energy_in.at[j - 1],
            send_sem=n_ss.at[j - 1],
            recv_sem=n_rs.at[j - 1],
            device_id={"ctx": me, "head": lax.rem(z + j, 4)},
        )

    def add_prior():
        @pl.loop(1, 8)
        def _(j):
            prior_in(j).wait_recv()

        sums = jnp.zeros((ROWS, HD), F32)
        for hd in range(8):
            cols = slice(hd * HD, (hd + 1) * HD)
            reach = dot3(q_lin[:, cols], entering[hd], (((1,), (0,)), ((), ())))
            linear = lin_out[:, cols] + jnp.exp(cum_col[:, hd : hd + 1]) * reach
            lin_out[:, cols] = linear
            sums = sums + linear * linear
        energy[...] = sums
        for j in range(1, 4):
            energy_out(j).start()

    def normalize():
        sums = energy[...]
        for j in range(1, 4):
            energy_out(j).wait_recv()
            sums = sums + energy_in[j - 1]
        total = jnp.sum(sums, axis=1, keepdims=True)
        ratio = jnp.broadcast_to(lax.rsqrt(total / (LH * HD) + EPSILON), (ROWS, HD))
        for hd in range(8):
            cols = slice(hd * HD, (hd + 1) * HD)
            lin_out[:, cols] = lin_out[:, cols] * ratio * gain[:, cols]

    def prepare(slot):
        part = kv.at[slot, 1 - core]
        remote(part, part, send.at[slot, 2], recv.at[slot, 1], targets[2]).wait_recv()
        for c in range(2):
            rows = slice(c * ROWS, (c + 1) * ROWS)
            high, low = halves(kv[slot, c, 0])
            k3[slot, rows, :HD] = high
            k3[slot, rows, HD : 2 * HD] = low
            k3[slot, rows, 2 * HD :] = high
            high, low = halves(kv[slot, c, 1])
            for copy in range(2):
                rows = slice(copy * KEYS + c * ROWS, copy * KEYS + (c + 1) * ROWS)
                v2[slot, rows, :HD] = high
                v2[slot, rows, HD:] = low

    def tile(g, slot, rows, ahead=None):
        scores = lax.dot_general(q3[g, rows, :], k3[slot], NT, preferred_element_type=F32)
        if ahead is not None:
            at = lax.broadcasted_iota(jnp.int32, (ROWS, KEYS), 0)
            key = lax.broadcasted_iota(jnp.int32, (ROWS, KEYS), 1)
            scores = jnp.where(key - at <= ahead * KEYS + core * ROWS, scores, NEGATIVE)
        before = m_all[g, rows, :]
        after = jnp.maximum(before, jnp.max(scores, axis=1, keepdims=True))
        weights = jnp.exp2(scores - jnp.concatenate([after] * (KEYS // HD), 1))
        shrink = jnp.exp2(before - after)
        sums = weights[:, :HD]
        for j in range(1, KEYS // HD):
            sums = sums + weights[:, j * HD : (j + 1) * HD]
        l_all[g, rows, :] = l_all[g, rows, :] * shrink + sums
        high, low = halves(weights)
        summed = jnp.dot(jnp.concatenate([high, low], 1), v2[slot], preferred_element_type=F32)
        acc[g, rows, :] = acc[g, rows, :] * jnp.concatenate([shrink, shrink], 1) + summed
        m_all[g, rows, :] = after

    def tile_rows(r):
        return slice(r * ROWS, (r + 1) * ROWS) if isinstance(r, int) else pl.ds(pl.multiple_of(r * ROWS, ROWS), ROWS)

    def result(g, r):
        rows = tile_rows(r)
        total = jnp.sum(l_all[g, rows, :], axis=1, keepdims=True)
        return (acc[g, rows, :HD] + acc[g, rows, HD:]) / total

    def o_out(r, col):
        cols = pl.ds(pl.multiple_of(col * GROUP * HD + r * HD, HD), HD)
        return remote(o_send.at[r], soft_out.at[:, cols], o_ss.at[r], o_rs.at[r], partner)

    def take_partner():
        swap_q.wait_recv()
        take_queries(1, q_in)

    def give_back():
        for r in range(GROUP):
            o_send[r] = result(1, r)
            o_out(r, half).start()

    def column(a):
        for dx in (3, 1, 2):
            arrive(a, dx)

    mine_at, partner_at = y * 4 + x, (3 - y) * 4 + x

    def finish():
        column(1)
        for dx in COLUMNS:
            prepare(4 + dx)
        column(3)

        @pl.when(present(3))
        def _():
            for dx in COLUMNS:
                prepare(12 + dx)

        @pl.loop(0, GROUP // 2)
        def _(pair):
            both = (2 * pair, 2 * pair + 1)
            for dx in COLUMNS:
                keys_at = (3 - y) * 4 + lax.rem(x + dx, 4)
                for r in both:
                    tile(1, 4 + dx, tile_rows(r), partner_at - keys_at)

            @pl.when(present(3))
            def _():
                for dx in COLUMNS:
                    for r in both:
                        tile(1, 12 + dx, tile_rows(r))

            for r in both:
                o_send[r] = result(1, r)
                o_out(r, half).start()

    events = (
        (0, 10, lambda: arrive(2, 0)),
        (6, 0, lambda: arrive(1, 0)),
        (1, 1, lambda: column(0)),
        (2, 2, combine_row),
        (8, 3, lambda: arrive(3, 0)),
        (99, 4, lambda: column(1)),
        (4, 8, take_partner),
        (8, 6, combine),
        (9, 20, lambda: column(2)),
        (12, 14, add_prior),
        (99, 12, lambda: column(3)),
        (15, 20, normalize),
        (99, 16, give_back),
        (16, 99, finish),
    )
    def pick(k, values):
        out = values[0]
        for at in range(1, len(values)):
            out = jnp.where(k == at, values[at], out)
        return out

    def table(k, column):
        return jnp.where(low, pick(k, [s[column] for s in LOW]), pick(k, [s[column] for s in HIGH]))

    @pl.loop(0, 24)
    def _(t):
        for at_low, at_high, act in events:
            pl.when(t == jnp.where(low, at_low, at_high))(act)

        k = lax.rem(t, 4)
        step = t // 4
        g, a = table(step, 0), table(step, 1)
        dx = pick(k, COLUMNS)
        slot = 4 * a + dx
        row = pick(a, ys)
        keys_at = row * 4 + lax.rem(x + dx, 4)
        asks = jnp.where(low & (t >= 16), -1, jnp.where(g == 0, mine_at, partner_at))
        here = pick(a, [present(p).astype(jnp.int32) for p in range(4)])

        @pl.when((table(step, 2) == 1) & (here == 1))
        def _():
            prepare(slot)

        @pl.when(keys_at < asks)
        def _():
            for r in range(GROUP):
                tile(g, slot, tile_rows(r))

        @pl.when(keys_at == asks)
        def _():
            for r in range(GROUP):
                tile(g, slot, tile_rows(r), 0)

    for r in range(GROUP):
        cols = pl.ds(pl.multiple_of(half * GROUP * HD + r * HD, HD), HD)
        soft_out[:, cols] = result(0, r)
    for r in range(GROUP):
        o_out(r, other).wait_recv()

    swap_k.wait_send()
    swap_v.wait_send()
    swap_q.wait_send()
    for a in range(4):
        for dx in range(4):
            for when, kind in onward(a, dx):
                guarded(when, lambda a=a, dx=dx, kind=kind: hop(a, dx, kind).wait_send())
    for r in range(GROUP):
        o_out(r, half).wait_send()
    for j in range(1, 4):
        energy_out(j).wait_send()

    @pl.loop(1, 8)
    def _(j):
        slice_out(j).wait_send()
        prior_out(j).wait_send()

    @pl.loop(1, 4)
    def _(j):
        total_out(j).wait_send()


def body(q_lin, k_lin, v_lin, log_decay, lin_gain, q_soft, k_soft, v_soft):
    vmem = pl.BlockSpec(memory_space=pltpu.VMEM)
    hbm = pl.BlockSpec(memory_space=pl.ANY)
    dma = pltpu.SemaphoreType.DMA
    return pl.pallas_call(
        kernel,
        out_shape=(
            jax.ShapeDtypeStruct(q_lin.shape, F32),
            jax.ShapeDtypeStruct(q_soft.shape, F32),
        ),
        in_specs=[hbm] * 3 + [vmem] * 2 + [hbm] * 3,
        out_specs=(vmem, vmem),
        scratch_shapes=[
            pltpu.VMEM((ROWS, 8 * HD), F32),
            pltpu.VMEM((ROWS, 8 * HD), F32),
            pltpu.VMEM((ROWS, 8 * HD), F32),
            pltpu.VMEM((16, 2, 2, ROWS, HD), F32),
            pltpu.VMEM((ROWS, GROUP * HD), F32),
            pltpu.VMEM((ROWS, GROUP * HD), F32),
            pltpu.VMEM((2, TILES, 3 * HD), BF16),
            pltpu.VMEM((16, KEYS, 3 * HD), BF16),
            pltpu.VMEM((16, 2 * KEYS, 2 * HD), BF16),
            pltpu.VMEM((2, TILES, HD), F32),
            pltpu.VMEM((2, TILES, HD), F32),
            pltpu.VMEM((2, TILES, 2 * HD), F32),
            pltpu.VMEM((GROUP, ROWS, HD), F32),
            pltpu.VMEM((8, HD + 8, HD), F32),
            pltpu.VMEM((8, HD + 8, HD), F32),
            pltpu.VMEM((8, HD, HD), F32),
            pltpu.VMEM((8, 8, HD), F32),
            pltpu.VMEM((HD + 8, HD), F32),
            pltpu.VMEM((4, HD + 8, HD), F32),
            pltpu.VMEM((8, HD, HD), F32),
            pltpu.VMEM((ROWS, HD), F32),
            pltpu.VMEM((3, ROWS, HD), F32),
            pltpu.VMEM((8, ROWS), F32),
            pltpu.VMEM((ROWS, 8), F32),
            dma((6,)), dma((3,)), dma((3,)), dma((16, 5)), dma((16, 2)), dma((GROUP,)), dma((GROUP,)),
            dma((8,)), dma((8,)), dma((4,)), dma((4,)), dma((8,)), dma((8,)), dma((3,)), dma((3,)),
        ],
        compiler_params=pltpu.CompilerParams(
            collective_id=0, has_side_effects=True, vmem_limit_bytes=60 << 20
        ),
        cost_estimate=pl.CostEstimate(
            flops=34 * 4 * TILES * ROWS * HD, bytes_accessed=12 << 20, transcendentals=34 * TILES * ROWS
        ),
        name="attention",
    )(q_lin, k_lin, v_lin, log_decay, lin_gain.reshape(1, -1), q_soft, k_soft, v_soft)


def solution(mesh):
    return jax.shard_map(
        body,
        mesh=mesh,
        in_specs=(
            P("ctx", "head"),
            P("ctx", "head"),
            P("ctx", "head"),
            P("head", "ctx"),
            P("head"),
            P("ctx", "head"),
            P("ctx", "head"),
            P("ctx", "head"),
        ),
        out_specs=(P("ctx", "head"), P("ctx", "head")),
        check_vma=False,
    )
```

```python
import functools
import math

import jax
import jax.numpy as jnp
from jax import lax
from jax.experimental import pallas as pl
from jax.experimental.pallas import tpu as pltpu
from jax.sharding import PartitionSpec as P

HD = 128
LH = 32
EPSILON = 1e-05
NEGATIVE = -1e30
F32 = jnp.float32
BF16 = jnp.bfloat16
NT = (((1,), (1,)), ((), ()))
TN = (((0,), (0,)), ((), ()))
ROWS = 256
KEYS = 512
GROUP = 6
TILES = GROUP * ROWS
COLUMNS = (0, 3, 1, 2)
LOW = ((0, 0, 1), (1, 0, 0), (0, 2, 1), (1, 2, 0), (0, 0, 0), (0, 0, 0))
HIGH = ((0, 0, 1), (0, 1, 1), (1, 1, 0), (1, 3, 1), (0, 3, 0), (0, 2, 1))


def halves(value):
    high = value.astype(BF16)
    return high, (value - high.astype(F32)).astype(BF16)


def dot3(left, right, dims):
    (la,), (ra,) = dims[0]
    lh, ll = halves(left)
    rh, rl = halves(right)
    return lax.dot_general(
        jnp.concatenate([lh, ll, lh], la),
        jnp.concatenate([rh, rh, rl], ra),
        dims,
        preferred_element_type=F32,
    )


def kernel(
    q_lin_all, k_lin_all, v_lin_all, log_decay, gain, q_soft, k_soft, v_soft,
    lin_out, soft_out,
    q_lin, k_lin, v_lin, kv, q_own, q_in, q3, k3, v2, m_all, l_all, acc, o_send,
    local, gathered, prior, reach_decay, row_out, row_in, entering, energy, energy_in, cum_row, cum_col,
    loaded, swap_send, swap_recv, send, recv, o_ss, o_rs, l_ss, l_rs, r_ss, r_rs, e_ss, e_rs, n_ss, n_rs,
):
    me = lax.axis_index("ctx")
    z = lax.axis_index("head")
    core, x, y = lax.rem(me, 2), lax.rem(me // 2, 4), me // 8
    half = y // 2
    other = 1 - half
    low, high_half = half == 0, half == 1
    inner = (y == 1) | (y == 2)
    always = y >= 0

    def device(yy, xx, cc):
        return (yy * 4 + xx) * 2 + cc

    y_pair = y + 1 - 2 * lax.rem(y, 2)
    ys = (y, 3 - y, y_pair, 3 - y_pair)
    right, left = lax.rem(x + 1, 4), lax.rem(x + 3, 4)
    partner = device(3 - y, x, core)
    across = lax.rem(x + 2, 4)
    targets = (
        device(y, right, core),
        device(y, left, core),
        device(y, x, 1 - core),
        device(y_pair, x, core),
        device(y, across, core),
    )

    def remote(src, dst, ss, rs, ctx):
        return pltpu.make_async_remote_copy(
            src_ref=src, dst_ref=dst, send_sem=ss, recv_sem=rs, device_id={"ctx": ctx, "head": z}
        )

    barrier = pltpu.get_barrier_semaphore()

    at_row = lax.rem(me, 8)
    row_start = me - at_row

    @pl.loop(1, 8)
    def _(j):
        pl.semaphore_signal(barrier, inc=1, device_id={"ctx": row_start + lax.rem(at_row + j, 8), "head": z})

    @pl.loop(1, 4)
    def _(j):
        pl.semaphore_signal(barrier, inc=1, device_id={"ctx": device(lax.rem(y + j, 4), x, core), "head": z})

    for j in range(1, 4):
        pl.semaphore_signal(barrier, inc=1, device_id={"ctx": me, "head": lax.rem(z + j, 4)})
    mine = pl.ds(pl.multiple_of(half * HD, HD), HD)
    others = pl.ds(pl.multiple_of(other * HD, HD), HD)
    loads = [
        pltpu.make_async_copy(k_soft.at[:, mine], kv.at[0, core, 0], loaded.at[0]),
        pltpu.make_async_copy(v_soft.at[:, mine], kv.at[0, core, 1], loaded.at[1]),
        pltpu.make_async_copy(q_lin_all, q_lin, loaded.at[2]),
        pltpu.make_async_copy(k_lin_all, k_lin, loaded.at[3]),
        pltpu.make_async_copy(v_lin_all, v_lin, loaded.at[4]),
        pltpu.make_async_copy(
            q_soft.at[:, pl.ds(pl.multiple_of(half * GROUP * HD, HD), GROUP * HD)], q_own, loaded.at[5]
        ),
    ]
    for load in loads:
        load.start()
    pl.semaphore_wait(barrier, 13)

    def hop(a, dx, kind):
        slot = 4 * a + dx
        to = {0: 4 * a + 3, 1: 4 * a + 1, 4: 4 * a + 2, 2: slot, 3: slot + 8}[kind]
        return remote(
            kv.at[slot, core], kv.at[to, core], send.at[slot, kind], recv.at[to, int(kind == 2)], targets[kind]
        )

    def present(a):
        return (always, always, jnp.logical_not(inner & high_half), jnp.logical_not(inner & low))[a]

    def onward(a, dx):
        out = []
        if a < 2:
            out.append((inner | (low, high_half)[a] if dx == 0 else inner, 3))
            if a == 1 and dx != 0:
                out = []
        if dx == 0:
            when = (always, always, inner & low, present(3))[a]
            out += [(when, 0), (when, 1), (when, 4)]
        return out + [(present(a), 2)]

    swap_k = remote(k_soft.at[:, others], kv.at[4, core, 0], swap_send.at[0], swap_recv.at[0], partner)
    swap_v = remote(v_soft.at[:, others], kv.at[4, core, 1], swap_send.at[2], swap_recv.at[2], partner)
    q_cols = pl.ds(pl.multiple_of(other * GROUP * HD, HD), GROUP * HD)
    swap_q = remote(q_soft.at[:, q_cols], q_in, swap_send.at[1], swap_recv.at[1], partner)

    def guarded(when, act):
        if when is always:
            act()
        else:
            pl.when(when)(act)

    def arrive(a, dx):
        slot = 4 * a + dx

        def wait():
            part = kv.at[slot, core]
            remote(part, part, send.at[slot, 0], recv.at[slot, 0], targets[2]).wait_recv()

        if (a, dx) == (1, 0):
            swap_k.wait_recv()
            swap_v.wait_recv()
        elif (a, dx) != (0, 0):
            guarded(present(a), wait)
        for when, kind in onward(a, dx):
            guarded(when, lambda kind=kind: hop(a, dx, kind).start())

    swap_k.start()
    swap_v.start()
    swap_q.start()
    loads[0].wait()
    loads[1].wait()
    arrive(0, 0)

    scale = math.log2(math.e) / math.sqrt(HD)

    def take_queries(g, ref):
        for r in range(GROUP):
            col = r * HD
            high, low = halves(ref[:, pl.ds(col, HD)] * scale)
            rows = slice(r * ROWS, (r + 1) * ROWS)
            q3[g, rows, :HD] = high
            q3[g, rows, HD : 2 * HD] = high
            q3[g, rows, 2 * HD :] = low

    m_all[...] = jnp.full_like(m_all, NEGATIVE)
    l_all[...] = jnp.zeros_like(l_all)
    acc[...] = jnp.zeros_like(acc)

    rates = log_decay[...]
    s_at = lax.broadcasted_iota(jnp.int32, (ROWS, ROWS), 0)
    t_at = lax.broadcasted_iota(jnp.int32, (ROWS, ROWS), 1)
    cum_row[...] = jnp.dot(
        rates, jnp.where(s_at <= t_at, 1.0, 0.0), precision=lax.Precision.HIGHEST, preferred_element_type=F32
    )
    cum_col[...] = cum_row[...].T

    def lightning_head(hd):
        cols = slice(hd * HD, (hd + 1) * HD)
        q, k, v = q_lin[:, cols], k_lin[:, cols], v_lin[:, cols]
        down = cum_col[:, hd : hd + 1]
        gaps = jnp.where(t_at <= s_at, down - cum_row[hd : hd + 1, :], NEGATIVE)
        scores = dot3(q, k, NT)
        lin_out[:, cols] = dot3(scores * jnp.exp(gaps), v, (((1,), (0,)), ((), ())))
        total = cum_col[ROWS - 1 : ROWS, hd : hd + 1]
        state = dot3(k * jnp.exp(total - down), v, TN)
        local[hd, :HD] = state
        local[hd, HD:] = jnp.broadcast_to(jnp.exp(total), (8, HD))

    for at in (2, 3, 4):
        loads[at].wait()
    for hd in range(8):
        lightning_head(hd)

    def slice_out(j):
        to = lax.rem(at_row + j, 8)
        return remote(local.at[to], gathered.at[at_row], l_ss.at[j], l_rs.at[j], row_start + to)

    def slice_in(j):
        come = lax.rem(at_row + 8 - j, 8)
        return remote(local.at[at_row], gathered.at[come], l_ss.at[j], l_rs.at[j], row_start + come)

    @pl.loop(1, 8)
    def _(j):
        slice_out(j).start()

    gathered[at_row] = local[at_row]
    loads[5].wait()
    take_queries(0, q_own)

    def total_out(j):
        return remote(row_out, row_in.at[y], r_ss.at[j], r_rs.at[j], device(lax.rem(y + j, 4), x, core))

    def total_in(j):
        come = lax.rem(y + 4 - j, 4)
        return remote(row_out, row_in.at[come], r_ss.at[j], r_rs.at[j], device(come, x, core))

    def combine_row():
        @pl.loop(1, 8)
        def _(j):
            slice_in(j).wait_recv()

        decay = jnp.ones((8, HD), F32)
        state = jnp.zeros((HD, HD), F32)
        for i in range(8):
            prior[i] = state
            reach_decay[i] = decay
            state = state * gathered[i, HD : HD + 1, :] + gathered[i, :HD]
            decay = decay * gathered[i, HD:, :]
        row_out[:HD] = state
        row_out[HD:] = decay

        @pl.loop(1, 4)
        def _(j):
            total_out(j).start()

    def prior_out(j):
        to = lax.rem(at_row + j, 8)
        return remote(prior.at[to], entering.at[at_row], e_ss.at[j], e_rs.at[j], row_start + to)

    def prior_in(j):
        come = lax.rem(at_row + 8 - j, 8)
        return remote(prior.at[at_row], entering.at[come], e_ss.at[j], e_rs.at[j], row_start + come)

    def combine():
        @pl.loop(1, 4)
        def _(j):
            total_in(j).wait_recv()

        row_in[y] = row_out[...]
        state = jnp.zeros((HD, HD), F32)
        for i in range(3):
            state = jnp.where(i < y, state * row_in[i, HD : HD + 1, :] + row_in[i, :HD], state)
        for i in range(8):
            prior[i] = prior[i] + reach_decay[i, :1, :] * state

        @pl.loop(1, 8)
        def _(j):
            prior_out(j).start()

        entering[at_row] = prior[at_row]

    def energy_out(j):
        return pltpu.make_async_remote_copy(
            src_ref=energy,
            dst_ref=energy_in.at[j - 1],
            send_sem=n_ss.at[j - 1],
            recv_sem=n_rs.at[j - 1],
            device_id={"ctx": me, "head": lax.rem(z + j, 4)},
        )

    def add_prior():
        @pl.loop(1, 8)
        def _(j):
            prior_in(j).wait_recv()

        sums = jnp.zeros((ROWS, HD), F32)
        for hd in range(8):
            cols = slice(hd * HD, (hd + 1) * HD)
            reach = dot3(q_lin[:, cols], entering[hd], (((1,), (0,)), ((), ())))
            linear = lin_out[:, cols] + jnp.exp(cum_col[:, hd : hd + 1]) * reach
            lin_out[:, cols] = linear
            sums = sums + linear * linear
        energy[...] = sums
        for j in range(1, 4):
            energy_out(j).start()

    def normalize():
        sums = energy[...]
        for j in range(1, 4):
            energy_out(j).wait_recv()
            sums = sums + energy_in[j - 1]
        total = jnp.sum(sums, axis=1, keepdims=True)
        ratio = jnp.broadcast_to(lax.rsqrt(total / (LH * HD) + EPSILON), (ROWS, HD))
        for hd in range(8):
            cols = slice(hd * HD, (hd + 1) * HD)
            lin_out[:, cols] = lin_out[:, cols] * ratio * gain[:, cols]

    def prepare(slot):
        part = kv.at[slot, 1 - core]
        remote(part, part, send.at[slot, 2], recv.at[slot, 1], targets[2]).wait_recv()
        for c in range(2):
            rows = slice(c * ROWS, (c + 1) * ROWS)
            high, low = halves(kv[slot, c, 0])
            k3[slot, rows, :HD] = high
            k3[slot, rows, HD : 2 * HD] = low
            k3[slot, rows, 2 * HD :] = high
            high, low = halves(kv[slot, c, 1])
            for copy in range(2):
                rows = slice(copy * KEYS + c * ROWS, copy * KEYS + (c + 1) * ROWS)
                v2[slot, rows, :HD] = high
                v2[slot, rows, HD:] = low

    def tile(g, slot, rows, ahead=None):
        scores = lax.dot_general(q3[g, rows, :], k3[slot], NT, preferred_element_type=F32)
        if ahead is not None:
            at = lax.broadcasted_iota(jnp.int32, (ROWS, KEYS), 0)
            key = lax.broadcasted_iota(jnp.int32, (ROWS, KEYS), 1)
            scores = jnp.where(key - at <= ahead * KEYS + core * ROWS, scores, NEGATIVE)
        before = m_all[g, rows, :]
        after = jnp.maximum(before, jnp.max(scores, axis=1, keepdims=True))
        weights = jnp.exp2(scores - jnp.concatenate([after] * (KEYS // HD), 1))
        shrink = jnp.exp2(before - after)
        sums = weights[:, :HD]
        for j in range(1, KEYS // HD):
            sums = sums + weights[:, j * HD : (j + 1) * HD]
        l_all[g, rows, :] = l_all[g, rows, :] * shrink + sums
        high, low = halves(weights)
        summed = jnp.dot(jnp.concatenate([high, low], 1), v2[slot], preferred_element_type=F32)
        acc[g, rows, :] = acc[g, rows, :] * jnp.concatenate([shrink, shrink], 1) + summed
        m_all[g, rows, :] = after

    def tile_rows(r):
        return slice(r * ROWS, (r + 1) * ROWS) if isinstance(r, int) else pl.ds(pl.multiple_of(r * ROWS, ROWS), ROWS)

    def result(g, r):
        rows = tile_rows(r)
        total = jnp.sum(l_all[g, rows, :], axis=1, keepdims=True)
        return (acc[g, rows, :HD] + acc[g, rows, HD:]) / total

    def o_out(r, col):
        cols = pl.ds(pl.multiple_of(col * GROUP * HD + r * HD, HD), HD)
        return remote(o_send.at[r], soft_out.at[:, cols], o_ss.at[r], o_rs.at[r], partner)

    def take_partner():
        swap_q.wait_recv()
        take_queries(1, q_in)

    def give_back():
        for r in range(GROUP):
            o_send[r] = result(1, r)
            o_out(r, half).start()

    def column(a):
        for dx in (3, 1, 2):
            arrive(a, dx)

    mine_at, partner_at = y * 4 + x, (3 - y) * 4 + x

    def finish():
        column(1)
        for dx in COLUMNS:
            prepare(4 + dx)
        column(3)

        @pl.when(present(3))
        def _():
            for dx in COLUMNS:
                prepare(12 + dx)

        @pl.loop(0, GROUP // 2)
        def _(pair):
            pl.when(pair == 1)(add_prior)
            both = (2 * pair, 2 * pair + 1)
            for dx in COLUMNS:
                keys_at = (3 - y) * 4 + lax.rem(x + dx, 4)
                for r in both:
                    tile(1, 4 + dx, tile_rows(r), partner_at - keys_at)

            @pl.when(present(3))
            def _():
                for dx in COLUMNS:
                    for r in both:
                        tile(1, 12 + dx, tile_rows(r))

            for r in both:
                o_send[r] = result(1, r)
                o_out(r, half).start()

    events = (
        (0, 10, lambda: arrive(2, 0)),
        (1, 0, lambda: arrive(1, 0)),
        (1, 1, lambda: column(0)),
        (2, 3, lambda: arrive(3, 0)),
        (99, 4, lambda: column(1)),
        (4, 8, take_partner),
        (4, 5, combine_row),
        (9, 20, lambda: column(2)),
        (12, 12, combine),
        (99, 12, lambda: column(3)),
        (99, 17, add_prior),
        (99, 16, give_back),
        (16, 99, finish),
    )

    def pick(k, values):
        out = values[0]
        for at in range(1, len(values)):
            out = jnp.where(k == at, values[at], out)
        return out

    def table(k, column):
        return jnp.where(low, pick(k, [s[column] for s in LOW]), pick(k, [s[column] for s in HIGH]))

    @pl.loop(0, 24)
    def _(t):
        for at_low, at_high, act in events:
            pl.when(t == jnp.where(low, at_low, at_high))(act)

        k = lax.rem(t, 4)
        step = t // 4
        g, a = table(step, 0), table(step, 1)
        dx = pick(k, COLUMNS)
        slot = 4 * a + dx
        row = pick(a, ys)
        keys_at = row * 4 + lax.rem(x + dx, 4)
        asks = jnp.where(low & (t >= 16), -1, jnp.where(g == 0, mine_at, partner_at))
        here = pick(a, [present(p).astype(jnp.int32) for p in range(4)])

        @pl.when((table(step, 2) == 1) & (here == 1))
        def _():
            prepare(slot)

        @pl.when(keys_at < asks)
        def _():
            for r in range(GROUP):
                tile(g, slot, tile_rows(r))

        @pl.when(keys_at == asks)
        def _():
            for r in range(GROUP):
                tile(g, slot, tile_rows(r), 0)

    normalize()
    for r in range(GROUP):
        cols = pl.ds(pl.multiple_of(half * GROUP * HD + r * HD, HD), HD)
        soft_out[:, cols] = result(0, r)
    for r in range(GROUP):
        o_out(r, other).wait_recv()

    swap_k.wait_send()
    swap_v.wait_send()
    swap_q.wait_send()
    for a in range(4):
        for dx in range(4):
            for when, kind in onward(a, dx):
                guarded(when, lambda a=a, dx=dx, kind=kind: hop(a, dx, kind).wait_send())
    for r in range(GROUP):
        o_out(r, half).wait_send()
    for j in range(1, 4):
        energy_out(j).wait_send()

    @pl.loop(1, 8)
    def _(j):
        slice_out(j).wait_send()
        prior_out(j).wait_send()

    @pl.loop(1, 4)
    def _(j):
        total_out(j).wait_send()


def body(q_lin, k_lin, v_lin, log_decay, lin_gain, q_soft, k_soft, v_soft):
    vmem = pl.BlockSpec(memory_space=pltpu.VMEM)
    hbm = pl.BlockSpec(memory_space=pl.ANY)
    dma = pltpu.SemaphoreType.DMA
    return pl.pallas_call(
        kernel,
        out_shape=(
            jax.ShapeDtypeStruct(q_lin.shape, F32),
            jax.ShapeDtypeStruct(q_soft.shape, F32),
        ),
        in_specs=[hbm] * 3 + [vmem] * 2 + [hbm] * 3,
        out_specs=(vmem, vmem),
        scratch_shapes=[
            pltpu.VMEM((ROWS, 8 * HD), F32),
            pltpu.VMEM((ROWS, 8 * HD), F32),
            pltpu.VMEM((ROWS, 8 * HD), F32),
            pltpu.VMEM((16, 2, 2, ROWS, HD), F32),
            pltpu.VMEM((ROWS, GROUP * HD), F32),
            pltpu.VMEM((ROWS, GROUP * HD), F32),
            pltpu.VMEM((2, TILES, 3 * HD), BF16),
            pltpu.VMEM((16, KEYS, 3 * HD), BF16),
            pltpu.VMEM((16, 2 * KEYS, 2 * HD), BF16),
            pltpu.VMEM((2, TILES, HD), F32),
            pltpu.VMEM((2, TILES, HD), F32),
            pltpu.VMEM((2, TILES, 2 * HD), F32),
            pltpu.VMEM((GROUP, ROWS, HD), F32),
            pltpu.VMEM((8, HD + 8, HD), F32),
            pltpu.VMEM((8, HD + 8, HD), F32),
            pltpu.VMEM((8, HD, HD), F32),
            pltpu.VMEM((8, 8, HD), F32),
            pltpu.VMEM((HD + 8, HD), F32),
            pltpu.VMEM((4, HD + 8, HD), F32),
            pltpu.VMEM((8, HD, HD), F32),
            pltpu.VMEM((ROWS, HD), F32),
            pltpu.VMEM((3, ROWS, HD), F32),
            pltpu.VMEM((8, ROWS), F32),
            pltpu.VMEM((ROWS, 8), F32),
            dma((6,)), dma((3,)), dma((3,)), dma((16, 5)), dma((16, 2)), dma((GROUP,)), dma((GROUP,)),
            dma((8,)), dma((8,)), dma((4,)), dma((4,)), dma((8,)), dma((8,)), dma((3,)), dma((3,)),
        ],
        compiler_params=pltpu.CompilerParams(
            collective_id=0, has_side_effects=True, vmem_limit_bytes=60 << 20
        ),
        cost_estimate=pl.CostEstimate(
            flops=34 * 4 * TILES * ROWS * HD, bytes_accessed=12 << 20, transcendentals=34 * TILES * ROWS
        ),
        name="attention",
    )(q_lin, k_lin, v_lin, log_decay, lin_gain.reshape(1, -1), q_soft, k_soft, v_soft)


def solution(mesh):
    return jax.shard_map(
        body,
        mesh=mesh,
        in_specs=(
            P("ctx", "head"),
            P("ctx", "head"),
            P("ctx", "head"),
            P("head", "ctx"),
            P("head"),
            P("ctx", "head"),
            P("ctx", "head"),
            P("ctx", "head"),
        ),
        out_specs=(P("ctx", "head"), P("ctx", "head")),
        check_vma=False,
    )
```

```python
import functools
import math

import jax
import jax.numpy as jnp
from jax import lax
from jax.experimental import pallas as pl
from jax.experimental.pallas import tpu as pltpu
from jax.sharding import PartitionSpec as P

HD = 128
LH = 32
EPSILON = 1e-05
NEGATIVE = -1e30
F32 = jnp.float32
BF16 = jnp.bfloat16
NT = (((1,), (1,)), ((), ()))
TN = (((0,), (0,)), ((), ()))
ROWS = 256
KEYS = 512
GROUP = 6
TILES = GROUP * ROWS
COLUMNS = (0, 3, 1, 2)
SETS = (
    ((0, 0, 1), (1, 0, 0), (0, 2, 1), (0, 0, 0), (0, 0, 0), (0, 0, 0)),
    ((0, 0, 1), (1, 0, 0), (1, 1, 1), (0, 0, 0), (0, 0, 0), (0, 0, 0)),
    ((0, 0, 1), (0, 1, 1), (1, 1, 0), (1, 3, 1), (0, 3, 0), (0, 2, 1)),
)


def halves(value):
    high = value.astype(BF16)
    return high, (value - high.astype(F32)).astype(BF16)


def dot3(left, right, dims):
    (la,), (ra,) = dims[0]
    lh, ll = halves(left)
    rh, rl = halves(right)
    return lax.dot_general(
        jnp.concatenate([lh, ll, lh], la),
        jnp.concatenate([rh, rh, rl], ra),
        dims,
        preferred_element_type=F32,
    )


def kernel(
    q_lin_all, k_lin_all, v_lin_all, log_decay, gain, q_soft, k_soft, v_soft,
    lin_out, soft_out,
    q_lin, k_lin, v_lin, kv, q_own, q_in, q3, k3, v2, m_all, l_all, acc, o_send,
    local, gathered, prior, reach_decay, row_out, row_in, entering, energy, energy_in, cum_row, cum_col,
    loaded, swap_send, swap_recv, send, recv, o_ss, o_rs, l_ss, l_rs, r_ss, r_rs, e_ss, e_rs, n_ss, n_rs,
):
    me = lax.axis_index("ctx")
    z = lax.axis_index("head")
    core, x, y = lax.rem(me, 2), lax.rem(me // 2, 4), me // 8
    half = y // 2
    other = 1 - half
    low, high_half = half == 0, half == 1
    inner = (y == 1) | (y == 2)
    always = y >= 0

    def device(yy, xx, cc):
        return (yy * 4 + xx) * 2 + cc

    y_pair = y + 1 - 2 * lax.rem(y, 2)
    ys = (y, 3 - y, y_pair, 3 - y_pair)
    right, left = lax.rem(x + 1, 4), lax.rem(x + 3, 4)
    partner = device(3 - y, x, core)
    across = lax.rem(x + 2, 4)
    targets = (
        device(y, right, core),
        device(y, left, core),
        device(y, x, 1 - core),
        device(y_pair, x, core),
        device(y, across, core),
    )

    def remote(src, dst, ss, rs, ctx):
        return pltpu.make_async_remote_copy(
            src_ref=src, dst_ref=dst, send_sem=ss, recv_sem=rs, device_id={"ctx": ctx, "head": z}
        )

    barrier = pltpu.get_barrier_semaphore()

    at_row = lax.rem(me, 8)
    row_start = me - at_row

    @pl.loop(1, 8)
    def _(j):
        pl.semaphore_signal(barrier, inc=1, device_id={"ctx": row_start + lax.rem(at_row + j, 8), "head": z})

    @pl.loop(1, 4)
    def _(j):
        pl.semaphore_signal(barrier, inc=1, device_id={"ctx": device(lax.rem(y + j, 4), x, core), "head": z})

    for j in range(1, 4):
        pl.semaphore_signal(barrier, inc=1, device_id={"ctx": me, "head": lax.rem(z + j, 4)})
    mine = pl.ds(pl.multiple_of(half * HD, HD), HD)
    others = pl.ds(pl.multiple_of(other * HD, HD), HD)
    loads = [
        pltpu.make_async_copy(k_soft.at[:, mine], kv.at[0, core, 0], loaded.at[0]),
        pltpu.make_async_copy(v_soft.at[:, mine], kv.at[0, core, 1], loaded.at[1]),
        pltpu.make_async_copy(q_lin_all, q_lin, loaded.at[2]),
        pltpu.make_async_copy(k_lin_all, k_lin, loaded.at[3]),
        pltpu.make_async_copy(v_lin_all, v_lin, loaded.at[4]),
        pltpu.make_async_copy(
            q_soft.at[:, pl.ds(pl.multiple_of(half * GROUP * HD, HD), GROUP * HD)], q_own, loaded.at[5]
        ),
    ]
    for load in loads:
        load.start()
    pl.semaphore_wait(barrier, 13)

    def hop(a, dx, kind):
        slot = 4 * a + dx
        to = {0: 4 * a + 3, 1: 4 * a + 1, 4: 4 * a + 2, 2: slot, 3: slot + 8}[kind]
        return remote(
            kv.at[slot, core], kv.at[to, core], send.at[slot, kind], recv.at[to, int(kind == 2)], targets[kind]
        )

    def present(a):
        return (always, always, jnp.logical_not(inner & high_half), jnp.logical_not(inner & low))[a]

    def onward(a, dx):
        out = []
        if a < 2:
            out.append((inner | (low, high_half)[a] if dx == 0 else inner | low, 3))
            if a == 1 and dx != 0:
                out = []
        if dx == 0 and a != 2:
            when = present(a)
            out += [(when, 0), (when, 1), (when, 4)]
        return out + [(present(a), 2)]

    swap_k = remote(k_soft.at[:, others], kv.at[4, core, 0], swap_send.at[0], swap_recv.at[0], partner)
    swap_v = remote(v_soft.at[:, others], kv.at[4, core, 1], swap_send.at[2], swap_recv.at[2], partner)
    q_cols = pl.ds(pl.multiple_of(other * GROUP * HD, HD), GROUP * HD)
    swap_q = remote(q_soft.at[:, q_cols], q_in, swap_send.at[1], swap_recv.at[1], partner)

    def guarded(when, act):
        if when is always:
            act()
        else:
            pl.when(when)(act)

    def arrive(a, dx):
        slot = 4 * a + dx

        def wait():
            part = kv.at[slot, core]
            remote(part, part, send.at[slot, 0], recv.at[slot, 0], targets[2]).wait_recv()

        if (a, dx) == (1, 0):
            swap_k.wait_recv()
            swap_v.wait_recv()
        elif (a, dx) != (0, 0):
            guarded(present(a), wait)
        for when, kind in onward(a, dx):
            guarded(when, lambda kind=kind: hop(a, dx, kind).start())

    swap_k.start()
    swap_v.start()
    swap_q.start()
    loads[0].wait()
    loads[1].wait()
    arrive(0, 0)

    scale = math.log2(math.e) / math.sqrt(HD)

    def take_queries(g, ref):
        for r in range(GROUP):
            col = r * HD
            high, low = halves(ref[:, pl.ds(col, HD)] * scale)
            rows = slice(r * ROWS, (r + 1) * ROWS)
            q3[g, rows, :HD] = high
            q3[g, rows, HD : 2 * HD] = high
            q3[g, rows, 2 * HD :] = low

    m_all[...] = jnp.full_like(m_all, NEGATIVE)
    l_all[...] = jnp.zeros_like(l_all)
    acc[...] = jnp.zeros_like(acc)

    rates = log_decay[...]
    s_at = lax.broadcasted_iota(jnp.int32, (ROWS, ROWS), 0)
    t_at = lax.broadcasted_iota(jnp.int32, (ROWS, ROWS), 1)
    cum_row[...] = jnp.dot(
        rates, jnp.where(s_at <= t_at, 1.0, 0.0), precision=lax.Precision.HIGHEST, preferred_element_type=F32
    )
    cum_col[...] = cum_row[...].T

    def lightning_head(hd):
        cols = slice(hd * HD, (hd + 1) * HD)
        q, k, v = q_lin[:, cols], k_lin[:, cols], v_lin[:, cols]
        down = cum_col[:, hd : hd + 1]
        gaps = jnp.where(t_at <= s_at, down - cum_row[hd : hd + 1, :], NEGATIVE)
        scores = dot3(q, k, NT)
        lin_out[:, cols] = dot3(scores * jnp.exp(gaps), v, (((1,), (0,)), ((), ())))
        total = cum_col[ROWS - 1 : ROWS, hd : hd + 1]
        state = dot3(k * jnp.exp(total - down), v, TN)
        local[hd, :HD] = state
        local[hd, HD:] = jnp.broadcast_to(jnp.exp(total), (8, HD))

    for at in (2, 3, 4):
        loads[at].wait()
    for hd in range(8):
        lightning_head(hd)

    def slice_out(j):
        to = lax.rem(at_row + j, 8)
        return remote(local.at[to], gathered.at[at_row], l_ss.at[j], l_rs.at[j], row_start + to)

    def slice_in(j):
        come = lax.rem(at_row + 8 - j, 8)
        return remote(local.at[at_row], gathered.at[come], l_ss.at[j], l_rs.at[j], row_start + come)

    @pl.loop(1, 8)
    def _(j):
        slice_out(j).start()

    gathered[at_row] = local[at_row]
    loads[5].wait()
    take_queries(0, q_own)

    def total_out(j):
        return remote(row_out, row_in.at[y], r_ss.at[j], r_rs.at[j], device(lax.rem(y + j, 4), x, core))

    def total_in(j):
        come = lax.rem(y + 4 - j, 4)
        return remote(row_out, row_in.at[come], r_ss.at[j], r_rs.at[j], device(come, x, core))

    def combine_row():
        @pl.loop(1, 8)
        def _(j):
            slice_in(j).wait_recv()

        decay = jnp.ones((8, HD), F32)
        state = jnp.zeros((HD, HD), F32)
        for i in range(8):
            prior[i] = state
            reach_decay[i] = decay
            state = state * gathered[i, HD : HD + 1, :] + gathered[i, :HD]
            decay = decay * gathered[i, HD:, :]
        row_out[:HD] = state
        row_out[HD:] = decay

        @pl.loop(1, 4)
        def _(j):
            total_out(j).start()

    def prior_out(j):
        to = lax.rem(at_row + j, 8)
        return remote(prior.at[to], entering.at[at_row], e_ss.at[j], e_rs.at[j], row_start + to)

    def prior_in(j):
        come = lax.rem(at_row + 8 - j, 8)
        return remote(prior.at[at_row], entering.at[come], e_ss.at[j], e_rs.at[j], row_start + come)

    def combine():
        @pl.loop(1, 4)
        def _(j):
            total_in(j).wait_recv()

        row_in[y] = row_out[...]
        state = jnp.zeros((HD, HD), F32)
        for i in range(3):
            state = jnp.where(i < y, state * row_in[i, HD : HD + 1, :] + row_in[i, :HD], state)
        for i in range(8):
            prior[i] = prior[i] + reach_decay[i, :1, :] * state

        @pl.loop(1, 8)
        def _(j):
            prior_out(j).start()

        entering[at_row] = prior[at_row]

    def energy_out(j):
        return pltpu.make_async_remote_copy(
            src_ref=energy,
            dst_ref=energy_in.at[j - 1],
            send_sem=n_ss.at[j - 1],
            recv_sem=n_rs.at[j - 1],
            device_id={"ctx": me, "head": lax.rem(z + j, 4)},
        )

    def add_prior():
        @pl.loop(1, 8)
        def _(j):
            prior_in(j).wait_recv()

        sums = jnp.zeros((ROWS, HD), F32)
        for hd in range(8):
            cols = slice(hd * HD, (hd + 1) * HD)
            reach = dot3(q_lin[:, cols], entering[hd], (((1,), (0,)), ((), ())))
            linear = lin_out[:, cols] + jnp.exp(cum_col[:, hd : hd + 1]) * reach
            lin_out[:, cols] = linear
            sums = sums + linear * linear
        energy[...] = sums
        for j in range(1, 4):
            energy_out(j).start()

    def normalize():
        sums = energy[...]
        for j in range(1, 4):
            energy_out(j).wait_recv()
            sums = sums + energy_in[j - 1]
        total = jnp.sum(sums, axis=1, keepdims=True)
        ratio = jnp.broadcast_to(lax.rsqrt(total / (LH * HD) + EPSILON), (ROWS, HD))
        for hd in range(8):
            cols = slice(hd * HD, (hd + 1) * HD)
            lin_out[:, cols] = lin_out[:, cols] * ratio * gain[:, cols]

    def prepare(slot):
        part = kv.at[slot, 1 - core]
        remote(part, part, send.at[slot, 2], recv.at[slot, 1], targets[2]).wait_recv()
        for c in range(2):
            rows = slice(c * ROWS, (c + 1) * ROWS)
            high, low = halves(kv[slot, c, 0])
            k3[slot, rows, :HD] = high
            k3[slot, rows, HD : 2 * HD] = low
            k3[slot, rows, 2 * HD :] = high
            high, low = halves(kv[slot, c, 1])
            for copy in range(2):
                rows = slice(copy * KEYS + c * ROWS, copy * KEYS + (c + 1) * ROWS)
                v2[slot, rows, :HD] = high
                v2[slot, rows, HD:] = low

    def tile(g, slot, rows, ahead=None):
        scores = lax.dot_general(q3[g, rows, :], k3[slot], NT, preferred_element_type=F32)
        if ahead is not None:
            at = lax.broadcasted_iota(jnp.int32, (ROWS, KEYS), 0)
            key = lax.broadcasted_iota(jnp.int32, (ROWS, KEYS), 1)
            scores = jnp.where(key - at <= ahead * KEYS + core * ROWS, scores, NEGATIVE)
        before = m_all[g, rows, :]
        after = jnp.maximum(before, jnp.max(scores, axis=1, keepdims=True))
        weights = jnp.exp2(scores - jnp.concatenate([after] * (KEYS // HD), 1))
        shrink = jnp.exp2(before - after)
        sums = weights[:, :HD]
        for j in range(1, KEYS // HD):
            sums = sums + weights[:, j * HD : (j + 1) * HD]
        l_all[g, rows, :] = l_all[g, rows, :] * shrink + sums
        high, low = halves(weights)
        summed = jnp.dot(jnp.concatenate([high, low], 1), v2[slot], preferred_element_type=F32)
        acc[g, rows, :] = acc[g, rows, :] * jnp.concatenate([shrink, shrink], 1) + summed
        m_all[g, rows, :] = after

    def tile_rows(r):
        return slice(r * ROWS, (r + 1) * ROWS) if isinstance(r, int) else pl.ds(pl.multiple_of(r * ROWS, ROWS), ROWS)

    def result(g, r):
        rows = tile_rows(r)
        total = jnp.sum(l_all[g, rows, :], axis=1, keepdims=True)
        return (acc[g, rows, :HD] + acc[g, rows, HD:]) / total

    def o_out(r, col):
        cols = pl.ds(pl.multiple_of(col * GROUP * HD + r * HD, HD), HD)
        return remote(o_send.at[r], soft_out.at[:, cols], o_ss.at[r], o_rs.at[r], partner)

    def take_partner():
        swap_q.wait_recv()
        take_queries(1, q_in)

    def give_back():
        for r in range(GROUP):
            o_send[r] = result(1, r)
            o_out(r, half).start()

    def column(a):
        for dx in (3, 1, 2):
            arrive(a, dx)

    mine_at, partner_at = y * 4 + x, (3 - y) * 4 + x

    def by_kind(values):
        return jnp.where(low, jnp.where(inner, values[0], values[1]), values[2])

    outer = jnp.logical_not(inner)
    end_a = jnp.where(inner, 1, 3)
    end_row = jnp.where(inner, ys[1], ys[3])

    def finish():
        @pl.when(inner)
        def _():
            column(1)
            for dx in COLUMNS:
                prepare(4 + dx)

        @pl.when(outer)
        def _():
            column(3)
            for dx in COLUMNS:
                prepare(12 + dx)
            column(2)
            for dx in COLUMNS:
                prepare(8 + dx)

        @pl.loop(0, GROUP // 2)
        def _(pair):
            pl.when(pair == 1)(add_prior)
            both = (2 * pair, 2 * pair + 1)
            for dx in COLUMNS:
                keys_at = end_row * 4 + lax.rem(x + dx, 4)
                for r in both:
                    tile(1, 4 * end_a + dx, tile_rows(r), partner_at - keys_at)

            for dx in COLUMNS:
                for r in both:
                    tile(1, 8 + dx, tile_rows(r))

            for r in both:
                o_send[r] = result(1, r)
                o_out(r, half).start()

    events = (
        ((0, 0, 10), lambda: arrive(2, 0)),
        ((1, 1, 0), lambda: arrive(1, 0)),
        ((1, 1, 1), lambda: column(0)),
        ((2, 2, 3), lambda: arrive(3, 0)),
        ((99, 8, 4), lambda: column(1)),
        ((4, 4, 8), take_partner),
        ((4, 4, 5), combine_row),
        ((8, 99, 20), lambda: column(2)),
        ((11, 10, 12), combine),
        ((99, 99, 12), lambda: column(3)),
        ((99, 99, 17), add_prior),
        ((99, 99, 16), give_back),
        ((12, 12, 99), finish),
    )

    def pick(k, values):
        out = values[0]
        for at in range(1, len(values)):
            out = jnp.where(k == at, values[at], out)
        return out

    def table(k, column):
        return by_kind([pick(k, [s[column] for s in sets]) for sets in SETS])

    @pl.loop(0, 24)
    def _(t):
        for at, act in events:
            pl.when(t == by_kind(at))(act)

        k = lax.rem(t, 4)
        step = t // 4
        g, a = table(step, 0), table(step, 1)
        dx = pick(k, COLUMNS)
        slot = 4 * a + dx
        row = pick(a, ys)
        keys_at = row * 4 + lax.rem(x + dx, 4)
        asks = jnp.where(low & (t >= 12), -1, jnp.where(g == 0, mine_at, partner_at))
        here = pick(a, [present(p).astype(jnp.int32) for p in range(4)])

        @pl.when((table(step, 2) == 1) & (here == 1))
        def _():
            prepare(slot)

        @pl.when(keys_at < asks)
        def _():
            for r in range(GROUP):
                tile(g, slot, tile_rows(r))

        @pl.when(keys_at == asks)
        def _():
            for r in range(GROUP):
                tile(g, slot, tile_rows(r), 0)

    normalize()
    for r in range(GROUP):
        cols = pl.ds(pl.multiple_of(half * GROUP * HD + r * HD, HD), HD)
        soft_out[:, cols] = result(0, r)
    for r in range(GROUP):
        o_out(r, other).wait_recv()

    swap_k.wait_send()
    swap_v.wait_send()
    swap_q.wait_send()
    for a in range(4):
        for dx in range(4):
            for when, kind in onward(a, dx):
                guarded(when, lambda a=a, dx=dx, kind=kind: hop(a, dx, kind).wait_send())
    for r in range(GROUP):
        o_out(r, half).wait_send()
    for j in range(1, 4):
        energy_out(j).wait_send()

    @pl.loop(1, 8)
    def _(j):
        slice_out(j).wait_send()
        prior_out(j).wait_send()

    @pl.loop(1, 4)
    def _(j):
        total_out(j).wait_send()


def body(q_lin, k_lin, v_lin, log_decay, lin_gain, q_soft, k_soft, v_soft):
    vmem = pl.BlockSpec(memory_space=pltpu.VMEM)
    hbm = pl.BlockSpec(memory_space=pl.ANY)
    dma = pltpu.SemaphoreType.DMA
    return pl.pallas_call(
        kernel,
        out_shape=(
            jax.ShapeDtypeStruct(q_lin.shape, F32),
            jax.ShapeDtypeStruct(q_soft.shape, F32),
        ),
        in_specs=[hbm] * 3 + [vmem] * 2 + [hbm] * 3,
        out_specs=(vmem, vmem),
        scratch_shapes=[
            pltpu.VMEM((ROWS, 8 * HD), F32),
            pltpu.VMEM((ROWS, 8 * HD), F32),
            pltpu.VMEM((ROWS, 8 * HD), F32),
            pltpu.VMEM((16, 2, 2, ROWS, HD), F32),
            pltpu.VMEM((ROWS, GROUP * HD), F32),
            pltpu.VMEM((ROWS, GROUP * HD), F32),
            pltpu.VMEM((2, TILES, 3 * HD), BF16),
            pltpu.VMEM((16, KEYS, 3 * HD), BF16),
            pltpu.VMEM((16, 2 * KEYS, 2 * HD), BF16),
            pltpu.VMEM((2, TILES, HD), F32),
            pltpu.VMEM((2, TILES, HD), F32),
            pltpu.VMEM((2, TILES, 2 * HD), F32),
            pltpu.VMEM((GROUP, ROWS, HD), F32),
            pltpu.VMEM((8, HD + 8, HD), F32),
            pltpu.VMEM((8, HD + 8, HD), F32),
            pltpu.VMEM((8, HD, HD), F32),
            pltpu.VMEM((8, 8, HD), F32),
            pltpu.VMEM((HD + 8, HD), F32),
            pltpu.VMEM((4, HD + 8, HD), F32),
            pltpu.VMEM((8, HD, HD), F32),
            pltpu.VMEM((ROWS, HD), F32),
            pltpu.VMEM((3, ROWS, HD), F32),
            pltpu.VMEM((8, ROWS), F32),
            pltpu.VMEM((ROWS, 8), F32),
            dma((6,)), dma((3,)), dma((3,)), dma((16, 5)), dma((16, 2)), dma((GROUP,)), dma((GROUP,)),
            dma((8,)), dma((8,)), dma((4,)), dma((4,)), dma((8,)), dma((8,)), dma((3,)), dma((3,)),
        ],
        compiler_params=pltpu.CompilerParams(
            collective_id=0, has_side_effects=True, vmem_limit_bytes=60 << 20
        ),
        cost_estimate=pl.CostEstimate(
            flops=34 * 4 * TILES * ROWS * HD, bytes_accessed=12 << 20, transcendentals=34 * TILES * ROWS
        ),
        name="attention",
    )(q_lin, k_lin, v_lin, log_decay, lin_gain.reshape(1, -1), q_soft, k_soft, v_soft)


def solution(mesh):
    return jax.shard_map(
        body,
        mesh=mesh,
        in_specs=(
            P("ctx", "head"),
            P("ctx", "head"),
            P("ctx", "head"),
            P("head", "ctx"),
            P("head"),
            P("ctx", "head"),
            P("ctx", "head"),
            P("ctx", "head"),
        ),
        out_specs=(P("ctx", "head"), P("ctx", "head")),
        check_vma=False,
    )
```

```python
import functools
import math

import jax
import jax.numpy as jnp
from jax import lax
from jax.experimental import pallas as pl
from jax.experimental.pallas import tpu as pltpu
from jax.sharding import PartitionSpec as P

HD = 128
LH = 32
EPSILON = 1e-05
NEGATIVE = -1e30
F32 = jnp.float32
BF16 = jnp.bfloat16
NT = (((1,), (1,)), ((), ()))
TN = (((0,), (0,)), ((), ()))
ROWS = 256
KEYS = 512
GROUP = 6
TILES = GROUP * ROWS
COLUMNS = (0, 3, 1, 2)
SETS = (
    ((0, 0, 1), (1, 0, 0), (0, 2, 1), (0, 0, 0), (0, 0, 0), (0, 0, 0)),
    ((0, 0, 1), (1, 0, 0), (1, 1, 1), (0, 0, 0), (0, 0, 0), (0, 0, 0)),
    ((0, 0, 1), (1, 1, 1), (1, 3, 1), (0, 1, 0), (0, 3, 0), (0, 2, 1)),
)


def halves(value):
    high = value.astype(BF16)
    return high, (value - high.astype(F32)).astype(BF16)


def dot3(left, right, dims):
    (la,), (ra,) = dims[0]
    lh, ll = halves(left)
    rh, rl = halves(right)
    return lax.dot_general(
        jnp.concatenate([lh, ll, lh], la),
        jnp.concatenate([rh, rh, rl], ra),
        dims,
        preferred_element_type=F32,
    )


def kernel(
    q_lin_all, k_lin_all, v_lin_all, log_decay, gain, q_soft, k_soft, v_soft,
    lin_out, soft_out,
    q_lin, k_lin, v_lin, kv, q_own, q_in, q3, k3, v2, m_all, l_all, acc, o_send,
    local, gathered, prior, reach_decay, row_out, row_in, entering, energy, energy_in, cum_row, cum_col,
    loaded, swap_send, swap_recv, send, recv, o_ss, o_rs, l_ss, l_rs, r_ss, r_rs, e_ss, e_rs, n_ss, n_rs,
):
    me = lax.axis_index("ctx")
    z = lax.axis_index("head")
    core, x, y = lax.rem(me, 2), lax.rem(me // 2, 4), me // 8
    half = y // 2
    other = 1 - half
    low, high_half = half == 0, half == 1
    inner = (y == 1) | (y == 2)
    always = y >= 0

    def device(yy, xx, cc):
        return (yy * 4 + xx) * 2 + cc

    y_pair = y + 1 - 2 * lax.rem(y, 2)
    ys = (y, 3 - y, y_pair, 3 - y_pair)
    right, left = lax.rem(x + 1, 4), lax.rem(x + 3, 4)
    partner = device(3 - y, x, core)
    across = lax.rem(x + 2, 4)
    targets = (
        device(y, right, core),
        device(y, left, core),
        device(y, x, 1 - core),
        device(y_pair, x, core),
        device(y, across, core),
    )

    def remote(src, dst, ss, rs, ctx):
        return pltpu.make_async_remote_copy(
            src_ref=src, dst_ref=dst, send_sem=ss, recv_sem=rs, device_id={"ctx": ctx, "head": z}
        )

    barrier = pltpu.get_barrier_semaphore()

    at_row = lax.rem(me, 8)
    row_start = me - at_row

    @pl.loop(1, 8)
    def _(j):
        pl.semaphore_signal(barrier, inc=1, device_id={"ctx": row_start + lax.rem(at_row + j, 8), "head": z})

    @pl.loop(1, 4)
    def _(j):
        pl.semaphore_signal(barrier, inc=1, device_id={"ctx": device(lax.rem(y + j, 4), x, core), "head": z})

    for j in range(1, 4):
        pl.semaphore_signal(barrier, inc=1, device_id={"ctx": me, "head": lax.rem(z + j, 4)})
    mine = pl.ds(pl.multiple_of(half * HD, HD), HD)
    others = pl.ds(pl.multiple_of(other * HD, HD), HD)
    loads = [
        pltpu.make_async_copy(k_soft.at[:, mine], kv.at[0, core, 0], loaded.at[0]),
        pltpu.make_async_copy(v_soft.at[:, mine], kv.at[0, core, 1], loaded.at[1]),
        pltpu.make_async_copy(q_lin_all, q_lin, loaded.at[2]),
        pltpu.make_async_copy(k_lin_all, k_lin, loaded.at[3]),
        pltpu.make_async_copy(v_lin_all, v_lin, loaded.at[4]),
        pltpu.make_async_copy(
            q_soft.at[:, pl.ds(pl.multiple_of(half * GROUP * HD, HD), GROUP * HD)], q_own, loaded.at[5]
        ),
    ]
    for load in loads:
        load.start()
    pl.semaphore_wait(barrier, 13)

    def hop(a, dx, kind):
        slot = 4 * a + dx
        to = {0: 4 * a + 3, 1: 4 * a + 1, 4: 4 * a + 2, 2: slot, 3: slot + 8}[kind]
        return remote(
            kv.at[slot, core], kv.at[to, core], send.at[slot, kind], recv.at[to, int(kind == 2)], targets[kind]
        )

    def present(a):
        return (always, always, jnp.logical_not(inner & high_half), jnp.logical_not(inner & low))[a]

    def onward(a, dx):
        out = []
        if a < 2:
            out.append((inner | (low, high_half)[a] if dx == 0 else inner | low, 3))
            if a == 1 and dx != 0:
                out = []
        if dx == 0 and a != 2:
            when = present(a)
            out += [(when, 0), (when, 1), (when, 4)]
        return out + [(present(a), 2)]

    swap_k = remote(k_soft.at[:, others], kv.at[4, core, 0], swap_send.at[0], swap_recv.at[0], partner)
    swap_v = remote(v_soft.at[:, others], kv.at[4, core, 1], swap_send.at[2], swap_recv.at[2], partner)
    q_cols = pl.ds(pl.multiple_of(other * GROUP * HD, HD), GROUP * HD)
    swap_q = remote(q_soft.at[:, q_cols], q_in, swap_send.at[1], swap_recv.at[1], partner)

    def guarded(when, act):
        if when is always:
            act()
        else:
            pl.when(when)(act)

    def arrive(a, dx):
        slot = 4 * a + dx

        def wait():
            part = kv.at[slot, core]
            remote(part, part, send.at[slot, 0], recv.at[slot, 0], targets[2]).wait_recv()

        if (a, dx) == (1, 0):
            swap_k.wait_recv()
            swap_v.wait_recv()
        elif (a, dx) != (0, 0):
            guarded(present(a), wait)
        for when, kind in onward(a, dx):
            guarded(when, lambda kind=kind: hop(a, dx, kind).start())

    swap_k.start()
    swap_v.start()
    swap_q.start()
    loads[0].wait()
    loads[1].wait()
    arrive(0, 0)

    scale = math.log2(math.e) / math.sqrt(HD)

    def take_queries(g, ref):
        for r in range(GROUP):
            col = r * HD
            high, low = halves(ref[:, pl.ds(col, HD)] * scale)
            rows = slice(r * ROWS, (r + 1) * ROWS)
            q3[g, rows, :HD] = high
            q3[g, rows, HD : 2 * HD] = high
            q3[g, rows, 2 * HD :] = low

    m_all[...] = jnp.full_like(m_all, NEGATIVE)
    l_all[...] = jnp.zeros_like(l_all)
    acc[...] = jnp.zeros_like(acc)

    rates = log_decay[...]
    s_at = lax.broadcasted_iota(jnp.int32, (ROWS, ROWS), 0)
    t_at = lax.broadcasted_iota(jnp.int32, (ROWS, ROWS), 1)
    cum_row[...] = jnp.dot(
        rates, jnp.where(s_at <= t_at, 1.0, 0.0), precision=lax.Precision.HIGHEST, preferred_element_type=F32
    )
    cum_col[...] = cum_row[...].T

    def lightning_head(hd):
        cols = slice(hd * HD, (hd + 1) * HD)
        q, k, v = q_lin[:, cols], k_lin[:, cols], v_lin[:, cols]
        down = cum_col[:, hd : hd + 1]
        gaps = jnp.where(t_at <= s_at, down - cum_row[hd : hd + 1, :], NEGATIVE)
        scores = dot3(q, k, NT)
        lin_out[:, cols] = dot3(scores * jnp.exp(gaps), v, (((1,), (0,)), ((), ())))
        total = cum_col[ROWS - 1 : ROWS, hd : hd + 1]
        state = dot3(k * jnp.exp(total - down), v, TN)
        local[hd, :HD] = state
        local[hd, HD:] = jnp.broadcast_to(jnp.exp(total), (8, HD))

    for at in (2, 3, 4):
        loads[at].wait()
    for hd in range(8):
        lightning_head(hd)

    def slice_out(j):
        to = lax.rem(at_row + j, 8)
        return remote(local.at[to], gathered.at[at_row], l_ss.at[j], l_rs.at[j], row_start + to)

    def slice_in(j):
        come = lax.rem(at_row + 8 - j, 8)
        return remote(local.at[at_row], gathered.at[come], l_ss.at[j], l_rs.at[j], row_start + come)

    @pl.loop(1, 8)
    def _(j):
        slice_out(j).start()

    gathered[at_row] = local[at_row]
    loads[5].wait()
    take_queries(0, q_own)

    def total_out(j):
        return remote(row_out, row_in.at[y], r_ss.at[j], r_rs.at[j], device(lax.rem(y + j, 4), x, core))

    def total_in(j):
        come = lax.rem(y + 4 - j, 4)
        return remote(row_out, row_in.at[come], r_ss.at[j], r_rs.at[j], device(come, x, core))

    def combine_row():
        @pl.loop(1, 8)
        def _(j):
            slice_in(j).wait_recv()

        decay = jnp.ones((8, HD), F32)
        state = jnp.zeros((HD, HD), F32)
        for i in range(8):
            prior[i] = state
            reach_decay[i] = decay
            state = state * gathered[i, HD : HD + 1, :] + gathered[i, :HD]
            decay = decay * gathered[i, HD:, :]
        row_out[:HD] = state
        row_out[HD:] = decay

        @pl.loop(1, 4)
        def _(j):
            total_out(j).start()

    def prior_out(j):
        to = lax.rem(at_row + j, 8)
        return remote(prior.at[to], entering.at[at_row], e_ss.at[j], e_rs.at[j], row_start + to)

    def prior_in(j):
        come = lax.rem(at_row + 8 - j, 8)
        return remote(prior.at[at_row], entering.at[come], e_ss.at[j], e_rs.at[j], row_start + come)

    def combine():
        @pl.loop(1, 4)
        def _(j):
            total_in(j).wait_recv()

        row_in[y] = row_out[...]
        state = jnp.zeros((HD, HD), F32)
        for i in range(3):
            state = jnp.where(i < y, state * row_in[i, HD : HD + 1, :] + row_in[i, :HD], state)
        for i in range(8):
            prior[i] = prior[i] + reach_decay[i, :1, :] * state

        @pl.loop(1, 8)
        def _(j):
            prior_out(j).start()

        entering[at_row] = prior[at_row]

    def energy_out(j):
        return pltpu.make_async_remote_copy(
            src_ref=energy,
            dst_ref=energy_in.at[j - 1],
            send_sem=n_ss.at[j - 1],
            recv_sem=n_rs.at[j - 1],
            device_id={"ctx": me, "head": lax.rem(z + j, 4)},
        )

    def add_prior():
        @pl.loop(1, 8)
        def _(j):
            prior_in(j).wait_recv()

        sums = jnp.zeros((ROWS, HD), F32)
        for hd in range(8):
            cols = slice(hd * HD, (hd + 1) * HD)
            reach = dot3(q_lin[:, cols], entering[hd], (((1,), (0,)), ((), ())))
            linear = lin_out[:, cols] + jnp.exp(cum_col[:, hd : hd + 1]) * reach
            lin_out[:, cols] = linear
            sums = sums + linear * linear
        energy[...] = sums
        for j in range(1, 4):
            energy_out(j).start()

    def normalize():
        sums = energy[...]
        for j in range(1, 4):
            energy_out(j).wait_recv()
            sums = sums + energy_in[j - 1]
        total = jnp.sum(sums, axis=1, keepdims=True)
        ratio = jnp.broadcast_to(lax.rsqrt(total / (LH * HD) + EPSILON), (ROWS, HD))
        for hd in range(8):
            cols = slice(hd * HD, (hd + 1) * HD)
            lin_out[:, cols] = lin_out[:, cols] * ratio * gain[:, cols]

    def prepare(slot):
        part = kv.at[slot, 1 - core]
        remote(part, part, send.at[slot, 2], recv.at[slot, 1], targets[2]).wait_recv()
        for c in range(2):
            rows = slice(c * ROWS, (c + 1) * ROWS)
            high, low = halves(kv[slot, c, 0])
            k3[slot, rows, :HD] = high
            k3[slot, rows, HD : 2 * HD] = low
            k3[slot, rows, 2 * HD :] = high
            high, low = halves(kv[slot, c, 1])
            for copy in range(2):
                rows = slice(copy * KEYS + c * ROWS, copy * KEYS + (c + 1) * ROWS)
                v2[slot, rows, :HD] = high
                v2[slot, rows, HD:] = low

    def tile(g, slot, rows, ahead=None):
        scores = lax.dot_general(q3[g, rows, :], k3[slot], NT, preferred_element_type=F32)
        if ahead is not None:
            at = lax.broadcasted_iota(jnp.int32, (ROWS, KEYS), 0)
            key = lax.broadcasted_iota(jnp.int32, (ROWS, KEYS), 1)
            scores = jnp.where(key - at <= ahead * KEYS + core * ROWS, scores, NEGATIVE)
        before = m_all[g, rows, :]
        after = jnp.maximum(before, jnp.max(scores, axis=1, keepdims=True))
        weights = jnp.exp2(scores - jnp.concatenate([after] * (KEYS // HD), 1))
        shrink = jnp.exp2(before - after)
        sums = weights[:, :HD]
        for j in range(1, KEYS // HD):
            sums = sums + weights[:, j * HD : (j + 1) * HD]
        l_all[g, rows, :] = l_all[g, rows, :] * shrink + sums
        high, low = halves(weights)
        summed = jnp.dot(jnp.concatenate([high, low], 1), v2[slot], preferred_element_type=F32)
        acc[g, rows, :] = acc[g, rows, :] * jnp.concatenate([shrink, shrink], 1) + summed
        m_all[g, rows, :] = after

    def tile_rows(r):
        return slice(r * ROWS, (r + 1) * ROWS) if isinstance(r, int) else pl.ds(pl.multiple_of(r * ROWS, ROWS), ROWS)

    def result(g, r):
        rows = tile_rows(r)
        total = jnp.sum(l_all[g, rows, :], axis=1, keepdims=True)
        return (acc[g, rows, :HD] + acc[g, rows, HD:]) / total

    def o_out(r, col):
        cols = pl.ds(pl.multiple_of(col * GROUP * HD + r * HD, HD), HD)
        return remote(o_send.at[r], soft_out.at[:, cols], o_ss.at[r], o_rs.at[r], partner)

    def take_partner():
        swap_q.wait_recv()
        take_queries(1, q_in)

    def give_back():
        for r in range(GROUP):
            o_send[r] = result(1, r)
            o_out(r, half).start()

    def column(a):
        for dx in (3, 1, 2):
            arrive(a, dx)

    mine_at, partner_at = y * 4 + x, (3 - y) * 4 + x

    def by_kind(values):
        return jnp.where(low, jnp.where(inner, values[0], values[1]), values[2])

    outer = jnp.logical_not(inner)
    end_a = jnp.where(inner, 1, 3)
    end_row = jnp.where(inner, ys[1], ys[3])

    def finish():
        @pl.when(inner)
        def _():
            column(1)
            for dx in COLUMNS:
                prepare(4 + dx)

        @pl.when(outer)
        def _():
            column(3)
            for dx in COLUMNS:
                prepare(12 + dx)
            column(2)
            for dx in COLUMNS:
                prepare(8 + dx)

        @pl.loop(0, GROUP // 2)
        def _(pair):
            pl.when(pair == 1)(add_prior)
            both = (2 * pair, 2 * pair + 1)
            for dx in COLUMNS:
                keys_at = end_row * 4 + lax.rem(x + dx, 4)
                for r in both:
                    tile(1, 4 * end_a + dx, tile_rows(r), partner_at - keys_at)

            for dx in COLUMNS:
                for r in both:
                    tile(1, 8 + dx, tile_rows(r))

            for r in both:
                o_send[r] = result(1, r)
                o_out(r, half).start()

    events = (
        ((0, 0, 10), lambda: arrive(2, 0)),
        ((1, 1, 0), lambda: arrive(1, 0)),
        ((1, 1, 1), lambda: column(0)),
        ((2, 2, 3), lambda: arrive(3, 0)),
        ((99, 8, 4), lambda: column(1)),
        ((4, 4, 4), take_partner),
        ((4, 4, 5), combine_row),
        ((8, 99, 20), lambda: column(2)),
        ((11, 10, 12), combine),
        ((99, 99, 8), lambda: column(3)),
        ((99, 99, 17), add_prior),
        ((99, 99, 12), give_back),
        ((12, 12, 99), finish),
    )

    def pick(k, values):
        out = values[0]
        for at in range(1, len(values)):
            out = jnp.where(k == at, values[at], out)
        return out

    def table(k, column):
        return by_kind([pick(k, [s[column] for s in sets]) for sets in SETS])

    @pl.loop(0, 24)
    def _(t):
        for at, act in events:
            pl.when(t == by_kind(at))(act)

        k = lax.rem(t, 4)
        step = t // 4
        g, a = table(step, 0), table(step, 1)
        dx = pick(k, COLUMNS)
        slot = 4 * a + dx
        row = pick(a, ys)
        keys_at = row * 4 + lax.rem(x + dx, 4)
        asks = jnp.where(low & (t >= 12), -1, jnp.where(g == 0, mine_at, partner_at))
        here = pick(a, [present(p).astype(jnp.int32) for p in range(4)])

        @pl.when((table(step, 2) == 1) & (here == 1))
        def _():
            prepare(slot)

        @pl.when(keys_at < asks)
        def _():
            for r in range(GROUP):
                tile(g, slot, tile_rows(r))

        @pl.when(keys_at == asks)
        def _():
            for r in range(GROUP):
                tile(g, slot, tile_rows(r), 0)

    normalize()
    for r in range(GROUP):
        cols = pl.ds(pl.multiple_of(half * GROUP * HD + r * HD, HD), HD)
        soft_out[:, cols] = result(0, r)
    for r in range(GROUP):
        o_out(r, other).wait_recv()

    swap_k.wait_send()
    swap_v.wait_send()
    swap_q.wait_send()
    for a in range(4):
        for dx in range(4):
            for when, kind in onward(a, dx):
                guarded(when, lambda a=a, dx=dx, kind=kind: hop(a, dx, kind).wait_send())
    for r in range(GROUP):
        o_out(r, half).wait_send()
    for j in range(1, 4):
        energy_out(j).wait_send()

    @pl.loop(1, 8)
    def _(j):
        slice_out(j).wait_send()
        prior_out(j).wait_send()

    @pl.loop(1, 4)
    def _(j):
        total_out(j).wait_send()


def body(q_lin, k_lin, v_lin, log_decay, lin_gain, q_soft, k_soft, v_soft):
    vmem = pl.BlockSpec(memory_space=pltpu.VMEM)
    hbm = pl.BlockSpec(memory_space=pl.ANY)
    dma = pltpu.SemaphoreType.DMA
    return pl.pallas_call(
        kernel,
        out_shape=(
            jax.ShapeDtypeStruct(q_lin.shape, F32),
            jax.ShapeDtypeStruct(q_soft.shape, F32),
        ),
        in_specs=[hbm] * 3 + [vmem] * 2 + [hbm] * 3,
        out_specs=(vmem, vmem),
        scratch_shapes=[
            pltpu.VMEM((ROWS, 8 * HD), F32),
            pltpu.VMEM((ROWS, 8 * HD), F32),
            pltpu.VMEM((ROWS, 8 * HD), F32),
            pltpu.VMEM((16, 2, 2, ROWS, HD), F32),
            pltpu.VMEM((ROWS, GROUP * HD), F32),
            pltpu.VMEM((ROWS, GROUP * HD), F32),
            pltpu.VMEM((2, TILES, 3 * HD), BF16),
            pltpu.VMEM((16, KEYS, 3 * HD), BF16),
            pltpu.VMEM((16, 2 * KEYS, 2 * HD), BF16),
            pltpu.VMEM((2, TILES, HD), F32),
            pltpu.VMEM((2, TILES, HD), F32),
            pltpu.VMEM((2, TILES, 2 * HD), F32),
            pltpu.VMEM((GROUP, ROWS, HD), F32),
            pltpu.VMEM((8, HD + 8, HD), F32),
            pltpu.VMEM((8, HD + 8, HD), F32),
            pltpu.VMEM((8, HD, HD), F32),
            pltpu.VMEM((8, 8, HD), F32),
            pltpu.VMEM((HD + 8, HD), F32),
            pltpu.VMEM((4, HD + 8, HD), F32),
            pltpu.VMEM((8, HD, HD), F32),
            pltpu.VMEM((ROWS, HD), F32),
            pltpu.VMEM((3, ROWS, HD), F32),
            pltpu.VMEM((8, ROWS), F32),
            pltpu.VMEM((ROWS, 8), F32),
            dma((6,)), dma((3,)), dma((3,)), dma((16, 5)), dma((16, 2)), dma((GROUP,)), dma((GROUP,)),
            dma((8,)), dma((8,)), dma((4,)), dma((4,)), dma((8,)), dma((8,)), dma((3,)), dma((3,)),
        ],
        compiler_params=pltpu.CompilerParams(
            collective_id=0, has_side_effects=True, vmem_limit_bytes=60 << 20
        ),
        cost_estimate=pl.CostEstimate(
            flops=34 * 4 * TILES * ROWS * HD, bytes_accessed=12 << 20, transcendentals=34 * TILES * ROWS
        ),
        name="attention",
    )(q_lin, k_lin, v_lin, log_decay, lin_gain.reshape(1, -1), q_soft, k_soft, v_soft)


def solution(mesh):
    return jax.shard_map(
        body,
        mesh=mesh,
        in_specs=(
            P("ctx", "head"),
            P("ctx", "head"),
            P("ctx", "head"),
            P("head", "ctx"),
            P("head"),
            P("ctx", "head"),
            P("ctx", "head"),
            P("ctx", "head"),
        ),
        out_specs=(P("ctx", "head"), P("ctx", "head")),
        check_vma=False,
    )
```

```python
import functools
import math

import jax
import jax.numpy as jnp
from jax import lax
from jax.experimental import pallas as pl
from jax.experimental.pallas import tpu as pltpu
from jax.sharding import PartitionSpec as P

HD = 128
LH = 32
EPSILON = 1e-05
NEGATIVE = -1e30
F32 = jnp.float32
BF16 = jnp.bfloat16
NT = (((1,), (1,)), ((), ()))
TN = (((0,), (0,)), ((), ()))
ROWS = 256
KEYS = 512
GROUP = 6
TILES = GROUP * ROWS
COLUMNS = (0, 3, 1, 2)
SETS = (
    ((0, 0, 1), (1, 0, 0), (0, 2, 1), (0, 0, 0), (0, 0, 0), (0, 0, 0)),
    ((0, 0, 1), (1, 0, 0), (1, 1, 0), (0, 0, 0), (0, 0, 0), (0, 0, 0)),
    ((0, 0, 1), (1, 1, 0), (1, 3, 1), (0, 1, 0), (0, 3, 0), (0, 2, 1)),
)


def halves(value):
    high = value.astype(BF16)
    return high, (value - high.astype(F32)).astype(BF16)


def dot3(left, right, dims):
    (la,), (ra,) = dims[0]
    lh, ll = halves(left)
    rh, rl = halves(right)
    return lax.dot_general(
        jnp.concatenate([lh, ll, lh], la),
        jnp.concatenate([rh, rh, rl], ra),
        dims,
        preferred_element_type=F32,
    )


def kernel(
    q_lin_all, k_lin_all, v_lin_all, log_decay, gain, q_soft, k_soft, v_soft,
    lin_out, soft_out,
    q_lin, k_lin, v_lin, kv, q_own, q_in, q3, k3, v2, m_all, l_all, acc, o_send,
    local, gathered, prior, reach_decay, row_out, row_in, entering, energy, energy_in, cum_row, cum_col,
    loaded, swap_send, swap_recv, send, recv, o_ss, o_rs, l_ss, l_rs, r_ss, r_rs, e_ss, e_rs, n_ss, n_rs,
):
    me = lax.axis_index("ctx")
    z = lax.axis_index("head")
    core, x, y = lax.rem(me, 2), lax.rem(me // 2, 4), me // 8
    half = y // 2
    other = 1 - half
    low, high_half = half == 0, half == 1
    inner = (y == 1) | (y == 2)
    always = y >= 0

    def device(yy, xx, cc):
        return (yy * 4 + xx) * 2 + cc

    y_pair = y + 1 - 2 * lax.rem(y, 2)
    ys = (y, 3 - y, y_pair, 3 - y_pair)
    right, left = lax.rem(x + 1, 4), lax.rem(x + 3, 4)
    partner = device(3 - y, x, core)
    across = lax.rem(x + 2, 4)
    targets = (
        device(y, right, core),
        device(y, left, core),
        device(y, x, 1 - core),
        device(y_pair, x, core),
        device(y, across, core),
    )

    def remote(src, dst, ss, rs, ctx):
        return pltpu.make_async_remote_copy(
            src_ref=src, dst_ref=dst, send_sem=ss, recv_sem=rs, device_id={"ctx": ctx, "head": z}
        )

    barrier = pltpu.get_barrier_semaphore()

    at_row = lax.rem(me, 8)
    row_start = me - at_row

    @pl.loop(1, 8)
    def _(j):
        pl.semaphore_signal(barrier, inc=1, device_id={"ctx": row_start + lax.rem(at_row + j, 8), "head": z})

    @pl.loop(1, 4)
    def _(j):
        pl.semaphore_signal(barrier, inc=1, device_id={"ctx": device(lax.rem(y + j, 4), x, core), "head": z})

    for j in range(1, 4):
        pl.semaphore_signal(barrier, inc=1, device_id={"ctx": me, "head": lax.rem(z + j, 4)})
    mine = pl.ds(pl.multiple_of(half * HD, HD), HD)
    others = pl.ds(pl.multiple_of(other * HD, HD), HD)
    loads = [
        pltpu.make_async_copy(k_soft.at[:, mine], kv.at[0, core, 0], loaded.at[0]),
        pltpu.make_async_copy(v_soft.at[:, mine], kv.at[0, core, 1], loaded.at[1]),
        pltpu.make_async_copy(q_lin_all, q_lin, loaded.at[2]),
        pltpu.make_async_copy(k_lin_all, k_lin, loaded.at[3]),
        pltpu.make_async_copy(v_lin_all, v_lin, loaded.at[4]),
        pltpu.make_async_copy(
            q_soft.at[:, pl.ds(pl.multiple_of(half * GROUP * HD, HD), GROUP * HD)], q_own, loaded.at[5]
        ),
    ]
    for load in loads:
        load.start()
    pl.semaphore_wait(barrier, 13)

    def hop(a, dx, kind):
        slot = 4 * a + dx
        to = {0: 4 * a + 3, 1: 4 * a + 1, 4: 4 * a + 2, 2: slot, 3: slot + 8}[kind]
        return remote(
            kv.at[slot, core], kv.at[to, core], send.at[slot, kind], recv.at[to, int(kind == 2)], targets[kind]
        )

    def present(a):
        return (always, always, jnp.logical_not(inner & high_half), jnp.logical_not(inner & low))[a]

    def onward(a, dx):
        out = []
        if a < 2:
            out.append((inner | (low, high_half)[a] if dx == 0 else inner | low, 3))
            if a == 1 and dx != 0:
                out = []
        if dx == 0 and a != 2:
            when = present(a)
            out += [(when, 0), (when, 1), (when, 4)]
        return out + [(present(a), 2)]

    swap_k = remote(k_soft.at[:, others], kv.at[4, core, 0], swap_send.at[0], swap_recv.at[0], partner)
    swap_v = remote(v_soft.at[:, others], kv.at[4, core, 1], swap_send.at[2], swap_recv.at[2], partner)
    q_cols = pl.ds(pl.multiple_of(other * GROUP * HD, HD), GROUP * HD)
    swap_q = remote(q_soft.at[:, q_cols], q_in, swap_send.at[1], swap_recv.at[1], partner)

    def guarded(when, act):
        if when is always:
            act()
        else:
            pl.when(when)(act)

    def arrive(a, dx):
        slot = 4 * a + dx

        def wait():
            part = kv.at[slot, core]
            remote(part, part, send.at[slot, 0], recv.at[slot, 0], targets[2]).wait_recv()

        if (a, dx) == (1, 0):
            swap_k.wait_recv()
            swap_v.wait_recv()
        elif (a, dx) != (0, 0):
            guarded(present(a), wait)
        for when, kind in onward(a, dx):
            guarded(when, lambda kind=kind: hop(a, dx, kind).start())

    swap_k.start()
    swap_v.start()
    swap_q.start()
    loads[0].wait()
    loads[1].wait()
    arrive(0, 0)

    scale = math.log2(math.e) / math.sqrt(HD)

    def take_queries(g, ref):
        for r in range(GROUP):
            col = r * HD
            high, low = halves(ref[:, pl.ds(col, HD)] * scale)
            rows = slice(r * ROWS, (r + 1) * ROWS)
            q3[g, rows, :HD] = high
            q3[g, rows, HD : 2 * HD] = high
            q3[g, rows, 2 * HD :] = low

    m_all[...] = jnp.full_like(m_all, NEGATIVE)
    l_all[...] = jnp.zeros_like(l_all)
    acc[...] = jnp.zeros_like(acc)

    rates = log_decay[...]
    s_at = lax.broadcasted_iota(jnp.int32, (ROWS, ROWS), 0)
    t_at = lax.broadcasted_iota(jnp.int32, (ROWS, ROWS), 1)
    cum_row[...] = jnp.dot(
        rates, jnp.where(s_at <= t_at, 1.0, 0.0), precision=lax.Precision.HIGHEST, preferred_element_type=F32
    )
    cum_col[...] = cum_row[...].T

    def lightning_head(hd):
        cols = slice(hd * HD, (hd + 1) * HD)
        q, k, v = q_lin[:, cols], k_lin[:, cols], v_lin[:, cols]
        down = cum_col[:, hd : hd + 1]
        gaps = jnp.where(t_at <= s_at, down - cum_row[hd : hd + 1, :], NEGATIVE)
        scores = dot3(q, k, NT)
        lin_out[:, cols] = dot3(scores * jnp.exp(gaps), v, (((1,), (0,)), ((), ())))
        total = cum_col[ROWS - 1 : ROWS, hd : hd + 1]
        state = dot3(k * jnp.exp(total - down), v, TN)
        local[hd, :HD] = state
        local[hd, HD:] = jnp.broadcast_to(jnp.exp(total), (8, HD))

    for at in (2, 3, 4):
        loads[at].wait()
    for hd in range(8):
        lightning_head(hd)

    def slice_out(j):
        to = lax.rem(at_row + j, 8)
        return remote(local.at[to], gathered.at[at_row], l_ss.at[j], l_rs.at[j], row_start + to)

    def slice_in(j):
        come = lax.rem(at_row + 8 - j, 8)
        return remote(local.at[at_row], gathered.at[come], l_ss.at[j], l_rs.at[j], row_start + come)

    @pl.loop(1, 8)
    def _(j):
        slice_out(j).start()

    gathered[at_row] = local[at_row]
    loads[5].wait()
    take_queries(0, q_own)

    def total_out(j):
        return remote(row_out, row_in.at[y], r_ss.at[j], r_rs.at[j], device(lax.rem(y + j, 4), x, core))

    def total_in(j):
        come = lax.rem(y + 4 - j, 4)
        return remote(row_out, row_in.at[come], r_ss.at[j], r_rs.at[j], device(come, x, core))

    def combine_row():
        @pl.loop(1, 8)
        def _(j):
            slice_in(j).wait_recv()

        decay = jnp.ones((8, HD), F32)
        state = jnp.zeros((HD, HD), F32)
        for i in range(8):
            prior[i] = state
            reach_decay[i] = decay
            state = state * gathered[i, HD : HD + 1, :] + gathered[i, :HD]
            decay = decay * gathered[i, HD:, :]
        row_out[:HD] = state
        row_out[HD:] = decay

        @pl.loop(1, 4)
        def _(j):
            total_out(j).start()

    def prior_out(j):
        to = lax.rem(at_row + j, 8)
        return remote(prior.at[to], entering.at[at_row], e_ss.at[j], e_rs.at[j], row_start + to)

    def prior_in(j):
        come = lax.rem(at_row + 8 - j, 8)
        return remote(prior.at[at_row], entering.at[come], e_ss.at[j], e_rs.at[j], row_start + come)

    def combine():
        @pl.loop(1, 4)
        def _(j):
            total_in(j).wait_recv()

        row_in[y] = row_out[...]
        state = jnp.zeros((HD, HD), F32)
        for i in range(3):
            state = jnp.where(i < y, state * row_in[i, HD : HD + 1, :] + row_in[i, :HD], state)
        for i in range(8):
            prior[i] = prior[i] + reach_decay[i, :1, :] * state

        @pl.loop(1, 8)
        def _(j):
            prior_out(j).start()

        entering[at_row] = prior[at_row]

    def energy_out(j):
        return pltpu.make_async_remote_copy(
            src_ref=energy,
            dst_ref=energy_in.at[j - 1],
            send_sem=n_ss.at[j - 1],
            recv_sem=n_rs.at[j - 1],
            device_id={"ctx": me, "head": lax.rem(z + j, 4)},
        )

    def add_prior():
        @pl.loop(1, 8)
        def _(j):
            prior_in(j).wait_recv()

        sums = jnp.zeros((ROWS, HD), F32)
        for hd in range(8):
            cols = slice(hd * HD, (hd + 1) * HD)
            reach = dot3(q_lin[:, cols], entering[hd], (((1,), (0,)), ((), ())))
            linear = lin_out[:, cols] + jnp.exp(cum_col[:, hd : hd + 1]) * reach
            lin_out[:, cols] = linear
            sums = sums + linear * linear
        energy[...] = sums
        for j in range(1, 4):
            energy_out(j).start()

    def normalize():
        sums = energy[...]
        for j in range(1, 4):
            energy_out(j).wait_recv()
            sums = sums + energy_in[j - 1]
        total = jnp.sum(sums, axis=1, keepdims=True)
        ratio = jnp.broadcast_to(lax.rsqrt(total / (LH * HD) + EPSILON), (ROWS, HD))
        for hd in range(8):
            cols = slice(hd * HD, (hd + 1) * HD)
            lin_out[:, cols] = lin_out[:, cols] * ratio * gain[:, cols]

    def prepare(slot):
        part = kv.at[slot, 1 - core]
        remote(part, part, send.at[slot, 2], recv.at[slot, 1], targets[2]).wait_recv()
        for c in range(2):
            rows = slice(c * ROWS, (c + 1) * ROWS)
            high, low = halves(kv[slot, c, 0])
            k3[slot, rows, :HD] = high
            k3[slot, rows, HD : 2 * HD] = low
            k3[slot, rows, 2 * HD :] = high
            high, low = halves(kv[slot, c, 1])
            for copy in range(2):
                rows = slice(copy * KEYS + c * ROWS, copy * KEYS + (c + 1) * ROWS)
                v2[slot, rows, :HD] = high
                v2[slot, rows, HD:] = low

    def tile(g, slot, rows, ahead=None):
        scores = lax.dot_general(q3[g, rows, :], k3[slot], NT, preferred_element_type=F32)
        if ahead is not None:
            at = lax.broadcasted_iota(jnp.int32, (ROWS, KEYS), 0)
            key = lax.broadcasted_iota(jnp.int32, (ROWS, KEYS), 1)
            scores = jnp.where(key - at <= ahead * KEYS + core * ROWS, scores, NEGATIVE)
        before = m_all[g, rows, :]
        after = jnp.maximum(before, jnp.max(scores, axis=1, keepdims=True))
        weights = jnp.exp2(scores - jnp.concatenate([after] * (KEYS // HD), 1))
        shrink = jnp.exp2(before - after)
        sums = weights[:, :HD]
        for j in range(1, KEYS // HD):
            sums = sums + weights[:, j * HD : (j + 1) * HD]
        l_all[g, rows, :] = l_all[g, rows, :] * shrink + sums
        high, low = halves(weights)
        summed = jnp.dot(jnp.concatenate([high, low], 1), v2[slot], preferred_element_type=F32)
        acc[g, rows, :] = acc[g, rows, :] * jnp.concatenate([shrink, shrink], 1) + summed
        m_all[g, rows, :] = after

    def tile_rows(r):
        return slice(r * ROWS, (r + 1) * ROWS) if isinstance(r, int) else pl.ds(pl.multiple_of(r * ROWS, ROWS), ROWS)

    def result(g, r):
        rows = tile_rows(r)
        total = jnp.sum(l_all[g, rows, :], axis=1, keepdims=True)
        return (acc[g, rows, :HD] + acc[g, rows, HD:]) / total

    def o_out(r, col):
        cols = pl.ds(pl.multiple_of(col * GROUP * HD + r * HD, HD), HD)
        return remote(o_send.at[r], soft_out.at[:, cols], o_ss.at[r], o_rs.at[r], partner)

    def take_partner():
        swap_q.wait_recv()
        take_queries(1, q_in)

    def give_back():
        for r in range(GROUP):
            o_send[r] = result(1, r)
            o_out(r, half).start()

    def column(a):
        for dx in (3, 1, 2):
            arrive(a, dx)

    mine_at, partner_at = y * 4 + x, (3 - y) * 4 + x

    def by_kind(values):
        return jnp.where(low, jnp.where(inner, values[0], values[1]), values[2])

    outer = jnp.logical_not(inner)
    end_a = jnp.where(inner, 1, 3)
    end_row = jnp.where(inner, ys[1], ys[3])

    def take_row():
        column(1)
        for dx in COLUMNS:
            prepare(4 + dx)

    def finish():
        @pl.when(outer)
        def _():
            column(3)
            for dx in COLUMNS:
                prepare(12 + dx)
            column(2)
            for dx in COLUMNS:
                prepare(8 + dx)

        @pl.loop(0, GROUP // 2)
        def _(pair):
            pl.when(pair == 1)(add_prior)
            both = (2 * pair, 2 * pair + 1)
            for dx in COLUMNS:
                keys_at = end_row * 4 + lax.rem(x + dx, 4)
                for r in both:
                    tile(1, 4 * end_a + dx, tile_rows(r), partner_at - keys_at)

            for dx in COLUMNS:
                for r in both:
                    tile(1, 8 + dx, tile_rows(r))

            for r in both:
                o_send[r] = result(1, r)
                o_out(r, half).start()

    events = (
        ((0, 0, 10), lambda: arrive(2, 0)),
        ((1, 1, 0), lambda: arrive(1, 0)),
        ((1, 1, 1), lambda: column(0)),
        ((2, 2, 3), lambda: arrive(3, 0)),
        ((4, 4, 4), take_row),
        ((4, 4, 4), combine_row),
        ((4, 4, 4), take_partner),
        ((8, 99, 20), lambda: column(2)),
        ((11, 10, 12), combine),
        ((99, 99, 8), lambda: column(3)),
        ((99, 99, 17), add_prior),
        ((99, 99, 12), give_back),
        ((12, 12, 99), finish),
    )

    def pick(k, values):
        out = values[0]
        for at in range(1, len(values)):
            out = jnp.where(k == at, values[at], out)
        return out

    def table(k, column):
        return by_kind([pick(k, [s[column] for s in sets]) for sets in SETS])

    @pl.loop(0, 24)
    def _(t):
        for at, act in events:
            pl.when(t == by_kind(at))(act)

        k = lax.rem(t, 4)
        step = t // 4
        g, a = table(step, 0), table(step, 1)
        dx = pick(k, COLUMNS)
        slot = 4 * a + dx
        row = pick(a, ys)
        keys_at = row * 4 + lax.rem(x + dx, 4)
        asks = jnp.where(low & (t >= 12), -1, jnp.where(g == 0, mine_at, partner_at))
        here = pick(a, [present(p).astype(jnp.int32) for p in range(4)])

        @pl.when((table(step, 2) == 1) & (here == 1))
        def _():
            prepare(slot)

        @pl.when(keys_at < asks)
        def _():
            for r in range(GROUP):
                tile(g, slot, tile_rows(r))

        @pl.when(keys_at == asks)
        def _():
            for r in range(GROUP):
                tile(g, slot, tile_rows(r), 0)

    normalize()
    for r in range(GROUP):
        cols = pl.ds(pl.multiple_of(half * GROUP * HD + r * HD, HD), HD)
        soft_out[:, cols] = result(0, r)
    for r in range(GROUP):
        o_out(r, other).wait_recv()

    swap_k.wait_send()
    swap_v.wait_send()
    swap_q.wait_send()
    for a in range(4):
        for dx in range(4):
            for when, kind in onward(a, dx):
                guarded(when, lambda a=a, dx=dx, kind=kind: hop(a, dx, kind).wait_send())
    for r in range(GROUP):
        o_out(r, half).wait_send()
    for j in range(1, 4):
        energy_out(j).wait_send()

    @pl.loop(1, 8)
    def _(j):
        slice_out(j).wait_send()
        prior_out(j).wait_send()

    @pl.loop(1, 4)
    def _(j):
        total_out(j).wait_send()


def body(q_lin, k_lin, v_lin, log_decay, lin_gain, q_soft, k_soft, v_soft):
    vmem = pl.BlockSpec(memory_space=pltpu.VMEM)
    hbm = pl.BlockSpec(memory_space=pl.ANY)
    dma = pltpu.SemaphoreType.DMA
    return pl.pallas_call(
        kernel,
        out_shape=(
            jax.ShapeDtypeStruct(q_lin.shape, F32),
            jax.ShapeDtypeStruct(q_soft.shape, F32),
        ),
        in_specs=[hbm] * 3 + [vmem] * 2 + [hbm] * 3,
        out_specs=(vmem, vmem),
        scratch_shapes=[
            pltpu.VMEM((ROWS, 8 * HD), F32),
            pltpu.VMEM((ROWS, 8 * HD), F32),
            pltpu.VMEM((ROWS, 8 * HD), F32),
            pltpu.VMEM((16, 2, 2, ROWS, HD), F32),
            pltpu.VMEM((ROWS, GROUP * HD), F32),
            pltpu.VMEM((ROWS, GROUP * HD), F32),
            pltpu.VMEM((2, TILES, 3 * HD), BF16),
            pltpu.VMEM((16, KEYS, 3 * HD), BF16),
            pltpu.VMEM((16, 2 * KEYS, 2 * HD), BF16),
            pltpu.VMEM((2, TILES, HD), F32),
            pltpu.VMEM((2, TILES, HD), F32),
            pltpu.VMEM((2, TILES, 2 * HD), F32),
            pltpu.VMEM((GROUP, ROWS, HD), F32),
            pltpu.VMEM((8, HD + 8, HD), F32),
            pltpu.VMEM((8, HD + 8, HD), F32),
            pltpu.VMEM((8, HD, HD), F32),
            pltpu.VMEM((8, 8, HD), F32),
            pltpu.VMEM((HD + 8, HD), F32),
            pltpu.VMEM((4, HD + 8, HD), F32),
            pltpu.VMEM((8, HD, HD), F32),
            pltpu.VMEM((ROWS, HD), F32),
            pltpu.VMEM((3, ROWS, HD), F32),
            pltpu.VMEM((8, ROWS), F32),
            pltpu.VMEM((ROWS, 8), F32),
            dma((6,)), dma((3,)), dma((3,)), dma((16, 5)), dma((16, 2)), dma((GROUP,)), dma((GROUP,)),
            dma((8,)), dma((8,)), dma((4,)), dma((4,)), dma((8,)), dma((8,)), dma((3,)), dma((3,)),
        ],
        compiler_params=pltpu.CompilerParams(
            collective_id=0, has_side_effects=True, vmem_limit_bytes=60 << 20
        ),
        cost_estimate=pl.CostEstimate(
            flops=34 * 4 * TILES * ROWS * HD, bytes_accessed=12 << 20, transcendentals=34 * TILES * ROWS
        ),
        name="attention",
    )(q_lin, k_lin, v_lin, log_decay, lin_gain.reshape(1, -1), q_soft, k_soft, v_soft)


def solution(mesh):
    return jax.shard_map(
        body,
        mesh=mesh,
        in_specs=(
            P("ctx", "head"),
            P("ctx", "head"),
            P("ctx", "head"),
            P("head", "ctx"),
            P("head"),
            P("ctx", "head"),
            P("ctx", "head"),
            P("ctx", "head"),
        ),
        out_specs=(P("ctx", "head"), P("ctx", "head")),
        check_vma=False,
    )
```
